32 devices in a mesh: seq: 8 (over y, x, core), fsdp: 4 (over z).
Axes of the slice: x: 2, y: 2, z: 4, core: 2. Of those that a mesh axis runs over, the one named last changes fastest.
Arguments:
- characters: bfloat16 [4, 4, 3840, 1600], P(None, 'fsdp', 'seq'), may hold values from -6 to 6
- lengths: int32 [4, 4, 16], P(None, 'fsdp'), may hold values from 1 to 3824, 3840 in all within a row
- cotangent: bfloat16 [4, 4, 3840, 1600], P(None, 'fsdp', 'seq'), may hold values from -6 to 6
- encproject: bfloat16 [1600, 800], P('fsdp'), may hold values from -0.21875 to 0.21875
- enckernel: bfloat16 [5, 800, 800], P(None, 'fsdp'), may hold values from -0.125 to 0.125
- encexpand: bfloat16 [800, 1600], P('fsdp'), may hold values from -0.3125 to 0.3125
- encwidegain: bfloat16 [1600], P('fsdp'), may hold values from 0.5 to 1.5
- encgains: bfloat16 [2, 800], P(None, 'fsdp'), may hold values from 0.5 to 1.5
- encwideshift: bfloat16 [2, 1600], P(None, 'fsdp'), may hold values from -3 to 3
- encshifts: bfloat16 [4, 800], P(None, 'fsdp'), may hold values from -3 to 3
- decproject: bfloat16 [1600, 800], P('fsdp'), may hold values from -0.21875 to 0.21875
- deckernel: bfloat16 [3, 800, 800], P(None, 'fsdp'), may hold values from -0.1875 to 0.1875
- decexpand: bfloat16 [800, 1600], P('fsdp'), may hold values from -0.3125 to 0.3125
- decwidegain: bfloat16 [1600], P('fsdp'), may hold values from 0.5 to 1.5
- decgains: bfloat16 [2, 800], P(None, 'fsdp'), may hold values from 0.5 to 1.5
- decwideshift: bfloat16 [2, 1600], P(None, 'fsdp'), may hold values from -3 to 3
- decshifts: bfloat16 [4, 800], P(None, 'fsdp'), may hold values from -3 to 3
Outputs:
- output: bfloat16 [4, 4, 3840, 1600], P(None, 'fsdp', 'seq')
- grad_characters: bfloat16 [4, 4, 3840, 1600], P(None, 'fsdp', 'seq')
- grad_encproject: float32 [1600, 800], P('fsdp')
- grad_enckernel: float32 [5, 800, 800], P(None, 'fsdp')
- grad_encexpand: float32 [800, 1600], P('fsdp')
- grad_encwidegain: float32 [1600], P('fsdp')
- grad_encgains: float32 [2, 800], P(None, 'fsdp')
- grad_encwideshift: float32 [2, 1600], P(None, 'fsdp')
- grad_encshifts: float32 [4, 800], P(None, 'fsdp')
- grad_decproject: float32 [1600, 800], P('fsdp')
- grad_deckernel: float32 [3, 800, 800], P(None, 'fsdp')
- grad_decexpand: float32 [800, 1600], P('fsdp')
- grad_decwidegain: float32 [1600], P('fsdp')
- grad_decgains: float32 [2, 800], P(None, 'fsdp')
- grad_decwideshift: float32 [2, 1600], P(None, 'fsdp')
- grad_decshifts: float32 [4, 800], P(None, 'fsdp')
The draws below stay inside these ranges and needn't reach their ends.
Inputs may be any that keep to these rules, and one draw needn't show every extreme that they name: Each row of 16 lengths sums to 3840, and its largest entry is 3824.
All inputs are finite; a program needn't handle non-finite values.
Results may differ from the reference program's by a relative error of at most 0.012.
Values may be sent and summed in bfloat16 or wider, within the bound.
No kernel may reach another device: no remote copies, remote signals or barrier semaphores. Data moves between devices by JAX's collectives and lax.ppermute only.
A program may use at most 384 MiB of HBM per device.

```python
import math
import jax
import jax.numpy as jnp
import numpy as np
from jax import lax

D = 1600
INNER = 800
ENC_TAPS = 5
ENC_DILATION = 8
DEC_TAPS = 3
DEC_DILATION = 16
MICRO = 4
DOCS = 16
GROUPS = 4
GROUP_TOK = 3840
LONGEST = 3824


def block_levels(rng, extent, cuts, low, top_value):
    gain, own = 1.0, jax.random.fold_in(rng, 6)
    for dim, parts in cuts:
        steps = jnp.exp(jax.random.uniform(jax.random.fold_in(own, dim), (parts,), jnp.float32, low / len(cuts), top_value / len(cuts)))
        gain = gain * jnp.repeat(steps, extent[dim] // parts).reshape([-1 if axis == dim else 1 for axis in range(len(extent))])
    return gain


def length_profile(amount, total, reach, skew):
    portions = [(1 << 20) // math.isqrt(grade ** skew) + 1 for grade in range(2, amount + 1)]
    surplus, counts = total - reach - (amount - 1), [1] * (amount - 1)
    while surplus > 0:
        candidates = [i for i in range(amount - 1) if counts[i] < reach]
        mass, left = sum([portions[i] for i in candidates]), surplus
        for i in candidates:
            more = min(reach - counts[i], max(1, left * portions[i] // mass), surplus)
            counts[i] = counts[i] + more
            surplus = surplus - more
    return np.array([reach] + counts)


def ragged_sizes(own_key, count, total, bound, skew):
    if count == 2:
        one = jax.random.randint(own_key, (), max(1, total - bound), min(bound, total - 1) + 1)
        return jnp.stack([one, total - one])
    sizes = jnp.asarray(length_profile(count, total, bound, skew), jnp.int32)
    pairs = (count - 1) // 2
    source_of, taker = sizes[1:1 + 2 * pairs:2], sizes[2:2 + 2 * pairs:2]
    slack = jnp.minimum(source_of - 1, bound - taker)
    shifted = jax.random.randint(jax.random.fold_in(own_key, 1), (pairs,), 0, 1 << 20) % (slack + 1)
    sizes = sizes.at[1:1 + 2 * pairs:2].set(source_of - shifted).at[2:2 + 2 * pairs:2].set(taker + shifted)
    return sizes[jax.random.permutation(jax.random.fold_in(own_key, 2), count)]


def gaussian(own_key, extent, deviation, limit, cuts=(), kind=jnp.bfloat16):
    entries = deviation * jax.random.normal(own_key, extent, jnp.float32)
    if cuts:
        entries = entries * block_levels(own_key, extent, cuts, -0.22, 0.18)
    return jnp.clip(entries, -limit, limit).astype(kind)


def setup_inputs(seed: int = 0) -> dict:
    key_of = jax.random.split(jax.random.key(seed), 18)
    characters = gaussian(key_of[0], (MICRO, GROUPS, GROUP_TOK, D), 1.0, 6.0, ((1, 4), (2, 8)))
    lengths = jax.vmap(lambda own: ragged_sizes(own, DOCS, GROUP_TOK, LONGEST, 2))(jax.random.split(key_of[1], MICRO * GROUPS)).reshape((MICRO, GROUPS, DOCS)).astype(jnp.int32)
    cotangent = gaussian(key_of[2], (MICRO, GROUPS, GROUP_TOK, D), 1.0, 6.0, ((1, 4), (2, 8)))
    encproject = gaussian(key_of[3], (D, INNER), (D // 2) ** -0.5, 0.21875, ((0, 4),))
    enckernel = gaussian(key_of[4], (ENC_TAPS, INNER, INNER), (ENC_TAPS * INNER // 2) ** -0.5, 0.125, ((1, 4),))
    encexpand = gaussian(key_of[5], (INNER, D), (INNER // 2) ** -0.5, 0.3125, ((0, 4),))
    encwidegain = jnp.clip(1.0 + 0.1 * jax.random.normal(key_of[6], (D,), jnp.float32), 0.5, 1.5).astype(jnp.bfloat16)
    encgains = jnp.clip(1.0 + 0.1 * jax.random.normal(key_of[7], (2, INNER), jnp.float32), 0.5, 1.5).astype(jnp.bfloat16)
    encwideshift = gaussian(key_of[8], (2, D), 0.5, 3.0, ((1, 4),))
    encshifts = gaussian(key_of[9], (4, INNER), 0.5, 3.0, ((1, 4),))
    decproject = gaussian(key_of[10], (D, INNER), (D // 2) ** -0.5, 0.21875, ((0, 4),))
    deckernel = gaussian(key_of[11], (DEC_TAPS, INNER, INNER), (DEC_TAPS * INNER // 2) ** -0.5, 0.1875, ((1, 4),))
    decexpand = gaussian(key_of[12], (INNER, D), (INNER // 2) ** -0.5, 0.3125, ((0, 4),))
    decwidegain = jnp.clip(1.0 + 0.1 * jax.random.normal(key_of[13], (D,), jnp.float32), 0.5, 1.5).astype(jnp.bfloat16)
    decgains = jnp.clip(1.0 + 0.1 * jax.random.normal(key_of[14], (2, INNER), jnp.float32), 0.5, 1.5).astype(jnp.bfloat16)
    decwideshift = gaussian(key_of[15], (2, D), 0.5, 3.0, ((1, 4),))
    decshifts = gaussian(key_of[16], (4, INNER), 0.5, 3.0, ((1, 4),))
    return dict(characters=characters, lengths=lengths, cotangent=cotangent, encproject=encproject, enckernel=enckernel, encexpand=encexpand, encwidegain=encwidegain, encgains=encgains, encwideshift=encwideshift, encshifts=encshifts, decproject=decproject, deckernel=deckernel, decexpand=decexpand, decwidegain=decwidegain, decgains=decgains, decwideshift=decwideshift, decshifts=decshifts)


epsilon = 1e-05
highest = lax.Precision.HIGHEST

@jax.custom_vjp
def low(v):
    return lax.optimization_barrier(v.astype(jnp.bfloat16)).astype(jnp.float32)

@jax.custom_vjp
def low_back(v):
    return v

def low_keep(v):
    return (low(v), None)

def low_pass(kept, grad):
    return (grad,)

def back_keep(v):
    return (v, None)

def back_low(kept, grad):
    return (low(grad),)
low.defvjp(low_keep, low_pass)
low_back.defvjp(back_keep, back_low)

def matmul(factor, matrix):
    return jnp.dot(factor, matrix, precision=highest, preferred_element_type=jnp.float32)

def norm_silu(values, norm_gain, norm_shift):
    average = lax.optimization_barrier(jnp.mean(values, axis=-1, keepdims=True))
    centred = values - average
    spread = lax.optimization_barrier(jnp.mean(centred * centred, axis=-1, keepdims=True))
    return jax.nn.silu(centred * lax.rsqrt(spread + epsilon) * norm_gain + norm_shift)

def owners(places, doc_ends):
    return lax.optimization_barrier(jnp.sum((places[:, None] >= doc_ends[None, :]).astype(jnp.int32), axis=1)).astype(jnp.int32)

def tap_offsets(encoder):
    if encoder:
        return [(tap_index - ENC_TAPS // 2) * ENC_DILATION for tap_index in range(ENC_TAPS)]
    return [(tap_index - DEC_TAPS + 1) * DEC_DILATION for tap_index in range(DEC_TAPS)]

def tap_columns(hidden_rows, doc_ends, offsets):
    stream_len = hidden_rows.shape[0]
    pad_rows = max(ENC_DILATION * (ENC_TAPS // 2), DEC_DILATION * (DEC_TAPS - 1))
    padded = jnp.pad(hidden_rows, ((pad_rows, pad_rows), (0, 0)))
    places = jnp.arange(stream_len, dtype=jnp.int32)
    own_doc = owners(places, doc_ends)
    pieces = []
    for offset in offsets:
        partner = (places + offset).astype(jnp.int32)
        usable = (partner >= 0) & (partner < stream_len) & (owners(partner, doc_ends) == own_doc)
        window = lax.slice_in_dim(padded, pad_rows + offset, pad_rows + offset + stream_len, axis=0)
        pieces.append(jnp.where(usable[:, None], window, jnp.zeros_like(window)))
    return jnp.concatenate(pieces, axis=1)

def block(stream, doc_ends, weights, encoder):
    project, kernel, expand, wide_gain, gains, wide_shift, shifts = weights
    first = low(norm_silu(stream, wide_gain, wide_shift[0]))
    hidden_in = low_back(matmul(first, project) + shifts[2])
    second = low(norm_silu(hidden_in, gains[0], shifts[0]))
    columns = tap_columns(second, doc_ends, tap_offsets(encoder))
    flat_kernel = kernel.reshape(kernel.shape[0] * kernel.shape[1], kernel.shape[2])
    mixed = low_back(matmul(columns, flat_kernel) + shifts[3])
    third = low(norm_silu(mixed, gains[1], shifts[1]))
    branch = low_back(matmul(third, expand) + wide_shift[1])
    return stream + branch

def add_arrays(first_arr, second_arr):
    return first_arr + second_arr

def reference(characters, lengths, cotangent, encproject, enckernel, encexpand, encwidegain, encgains, encwideshift, encshifts, decproject, deckernel, decexpand, decwidegain, decgains, decwideshift, decshifts):
    enc_params = tuple((param_arr.astype(jnp.float32) for param_arr in (encproject, enckernel, encexpand, encwidegain, encgains, encwideshift, encshifts)))
    dec_params = tuple((param_arr.astype(jnp.float32) for param_arr in (decproject, deckernel, decexpand, decwidegain, decgains, decwideshift, decshifts)))
    streams = characters.reshape(-1, GROUP_TOK, D).astype(jnp.float32)
    cotangents = cotangent.reshape(-1, GROUP_TOK, D).astype(jnp.float32)
    ends_all = jnp.cumsum(lengths.reshape(-1, DOCS), axis=1).astype(jnp.int32)

    def one_stream(running, item):
        stream, doc_ends, stream_cot = item

        def forward(stream_in, enc_weights, dec_weights):
            middle = block(stream_in, doc_ends, enc_weights, True)
            return block(middle, doc_ends, dec_weights, False)
        result, pullback = jax.vjp(forward, stream, enc_params, dec_params)
        grad_stream, grad_enc, grad_dec = pullback(stream_cot)
        running = jax.tree.map(add_arrays, running, (grad_enc, grad_dec))
        return (running, (result, grad_stream))
    start = (tuple((jnp.zeros(param_arr.shape, jnp.float32) for param_arr in enc_params)), tuple((jnp.zeros(param_arr.shape, jnp.float32) for param_arr in dec_params)))
    totals, (results, grads) = lax.scan(one_stream, start, (streams, ends_all, cotangents))
    factor = 1.0 / jnp.sqrt(jnp.float32(MICRO * GROUPS * GROUP_TOK))
    output = results.reshape(characters.shape).astype(jnp.bfloat16)
    grad_characters = grads.reshape(characters.shape).astype(jnp.bfloat16)
    grad_enc, grad_dec = totals
    grad_enc = tuple((entry * factor for entry in grad_enc))
    grad_dec = tuple((entry * factor for entry in grad_dec))
    return (output, grad_characters, grad_enc[0], grad_enc[1], grad_enc[2], grad_enc[3], grad_enc[4], grad_enc[5], grad_enc[6], grad_dec[0], grad_dec[1], grad_dec[2], grad_dec[3], grad_dec[4], grad_dec[5], grad_dec[6])
```

```python
import jax
import jax.numpy as jnp
from jax import lax
from jax.experimental import pallas as pl
from jax.experimental.pallas import tpu as pltpu
from jax.sharding import PartitionSpec as P

ENC_TAPS = 5
ENC_DILATION = 8
DEC_TAPS = 3
DEC_DILATION = 16
EPSILON = 1e-05
CHUNK = 48
VMEM_LIMIT = 60 * 1024 * 1024

BF16 = jnp.bfloat16
F32 = jnp.float32
NN = (((1,), (0,)), ((), ()))
NT = (((1,), (1,)), ((), ()))
TN = (((0,), (0,)), ((), ()))


def dot(left, right, dims):
    return lax.dot_general(left, right, dims, preferred_element_type=F32)


def tap_offsets(encoder):
    if encoder:
        return [(tap - ENC_TAPS // 2) * ENC_DILATION for tap in range(ENC_TAPS)]
    return [(tap - DEC_TAPS + 1) * DEC_DILATION for tap in range(DEC_TAPS)]


def normalized(values):
    average = jnp.mean(values, axis=-1, keepdims=True)
    centred = values - average
    scale = lax.rsqrt(jnp.mean(centred * centred, axis=-1, keepdims=True) + EPSILON)
    return centred * scale, scale


def logistic(inner):
    return 0.5 * jnp.tanh(0.5 * inner) + 0.5


def norm_silu(values, gain, shift):
    unit, _ = normalized(values)
    inner = unit * gain + shift
    return inner * logistic(inner)


def norm_silu_back(values, gain, shift, grad):
    unit, scale = normalized(values)
    inner = unit * gain + shift
    gate = logistic(inner)
    grad_inner = grad * (gate + inner * gate * (1.0 - gate))
    grad_unit = grad_inner * gain
    along = jnp.mean(grad_unit * unit, axis=-1, keepdims=True)
    level = jnp.mean(grad_unit, axis=-1, keepdims=True)
    grad_values = scale * (grad_unit - level - unit * along)
    return grad_values, grad_inner * unit, grad_inner


def fold_rows(values):
    total = values[0:8]
    for start in range(8, values.shape[0], 8):
        total = total + values[start : start + 8]
    return total


def by_chunks(row_count, body):
    for start in range(0, row_count, CHUNK):
        body(pl.ds(start, CHUNK))


def clear_first(*refs):
    @pl.when(pl.program_id(0) == 0)
    def _():
        for ref in refs:
            ref[...] = jnp.zeros_like(ref)


def at_last(body):
    pl.when(pl.program_id(0) == pl.num_programs(0) - 1)(body)


def fill_columns(columns, extended, masks, offsets, front, row_count):
    width = extended.shape[-1]
    for tap, offset in enumerate(offsets):
        window = extended[front + offset : front + offset + row_count, :]
        if offset != 0:
            window = window * masks[:, tap : tap + 1]
        columns[:, tap * width : (tap + 1) * width] = window


def enter_kernel(stream, project, wide, inner, first, hidden, second):
    row_count = stream.shape[0]

    def make_first(rows):
        values = stream[rows, :].astype(F32)
        first[rows, :] = norm_silu(values, wide[0:1, :], wide[1:2, :]).astype(BF16)

    by_chunks(row_count, make_first)
    hidden[...] = dot(first[...], project[...], NN) + inner[4:5, :]

    def make_second(rows):
        second[rows, :] = norm_silu(hidden[rows, :], inner[0:1, :], inner[2:3, :]).astype(BF16)

    by_chunks(row_count, make_second)


def fetch(sources, spots, target, semaphores):
    copies = [
        pltpu.make_async_copy(source, target.at[spot], semaphores.at[index])
        for index, (source, spot) in enumerate(zip(sources, spots))
    ]
    for copy in copies:
        copy.start()
    for copy in copies:
        copy.wait()


def fetch_shards(place, pieces, fsdp_count, landed, semaphores):
    seq_count = len(pieces) // 2
    half_count = fsdp_count // 2
    sources, spots = [], []
    for index, piece in enumerate(pieces):
        half, differs = index // seq_count, index % seq_count
        for within in range(half_count):
            shard = place[0] ^ (half * half_count + within)
            sources.append(piece.at[within])
            spots.append(shard * seq_count + (place[2] ^ differs))
    fetch(sources, spots, landed, semaphores)


class Shards:
    def __init__(self, landed, fsdp_count):
        self.landed, self.fsdp_count = landed, fsdp_count
        self.seq_count = landed.shape[0] // fsdp_count

    def spread(self, shard, start, rows, write):
        part, done = self.landed.shape[1], 0
        while done < rows:
            owner, local = (start + done) // part, (start + done) % part
            size = min(rows - done, part - local)
            write(done, self.landed[shard * self.seq_count + owner, local : local + size, :])
            done += size


def enter_encoder_kernel(parts, spacing, place, *refs):
    refs = list(refs)
    stream = refs.pop(0)
    pieces = [refs.pop(0) for _ in range(len(refs) - 8)]
    wide, inner, first, hidden, second, project, landed, semaphores = refs
    shard_rows = project.shape[0] * parts // len(pieces)

    @pl.when(pl.program_id(0) == 0)
    def _():
        spots = [
            (place[0] ^ (index // parts)) * parts + (place[1] ^ (index % parts))
            for index in range(len(pieces))
        ]
        fetch(pieces, spots, landed, semaphores)
        for index in range(len(pieces)):
            start = index // parts * shard_rows + index % parts * spacing
            project[start : start + landed.shape[1], :] = landed[index]

    enter_kernel(stream, project, wide, inner, first, hidden, second)


def unpack_kernel(shards, start, taps, kernel, flat):
    width = flat.shape[0]
    part = width // shards.fsdp_count
    for own in range(shards.fsdp_count):
        for tap in range(taps):

            def write(done, block):
                row = own * part + done
                size = block.shape[0]
                kernel[tap * width + row : tap * width + row + size, :] = block
                flat[row : row + size, tap * width : (tap + 1) * width] = block

            shards.spread(own, start + tap * part, part, write)


def unpack_expand(shards, start, expand):
    width = expand.shape[1] // 2
    part = expand.shape[0] // shards.fsdp_count
    for own in range(shards.fsdp_count):
        for half in range(2):

            def write(done, block):
                row = own * part + done
                expand[row : row + block.shape[0], half * width : (half + 1) * width] = block

            shards.spread(own, start + half * part, part, write)


def unpack_rows(shards, start, whole):
    part = whole.shape[0] // shards.fsdp_count
    for own in range(shards.fsdp_count):

        def write(done, block):
            row = own * part + done
            whole[row : row + block.shape[0], :] = block

        shards.spread(own, start, part, write)


def middle_kernel(offsets, fsdp_count, place, second_in, low, high, masks, stream, *refs):
    pieces, refs = refs[:-12], refs[-12:]
    enc_wide, enc_inner, mixed, third, middle, expand, flat = refs[:7]
    extended, columns, kernel, landed, semaphores = refs[7:]
    row_count = stream.shape[0]
    front = low.shape[0]

    @pl.when(pl.program_id(0) == 0)
    def _():
        fetch_shards(place, pieces, fsdp_count, landed, semaphores)
        shards = Shards(landed, fsdp_count)
        unpack_kernel(shards, 0, len(offsets), kernel, flat)
        unpack_expand(shards, kernel.shape[0] // fsdp_count, expand)

    extended[:front, :] = low[...]
    extended[front : front + row_count, :] = second_in[...]
    extended[front + row_count :, :] = high[...]
    fill_columns(columns, extended, masks, offsets, front, row_count)
    mixed[...] = dot(columns[...], kernel[...], NN) + enc_inner[5:6, :]

    def make_third(rows):
        third[rows, :] = norm_silu(mixed[rows, :], enc_inner[1:2, :], enc_inner[3:4, :]).astype(
            BF16
        )

    by_chunks(row_count, make_third)
    middle[...] = dot(third[...], expand[...], NN)

    def make_middle(rows):
        branch = middle[rows, :] + enc_wide[2:3, :]
        middle[rows, :] = stream[rows, :].astype(F32) + branch

    by_chunks(row_count, make_middle)


def enter_decoder_kernel(taps, fsdp_count, place, stream, *refs):
    pieces, refs = refs[:-11], refs[-11:]
    wide, inner, first, hidden, second, project, kernel, flat, expand, landed, semaphores = refs

    @pl.when(pl.program_id(0) == 0)
    def _():
        fetch_shards(place, pieces, fsdp_count, landed, semaphores)
        shards = Shards(landed, fsdp_count)
        start = project.shape[0] // fsdp_count
        unpack_rows(shards, 0, project)
        unpack_kernel(shards, start, taps, kernel, flat)
        unpack_expand(shards, start + kernel.shape[0] // fsdp_count, expand)

    enter_kernel(stream, project, wide, inner, first, hidden, second)


def turn_kernel(
    offsets,
    second,
    low,
    masks,
    cotangent,
    kernel,
    expand,
    inner,
    third,
    grad_mixed,
    grad_expand,
    sums_wide,
    sums_inner,
    extended,
    columns,
    mixed,
    grad_third,
    total,
):
    row_count = cotangent.shape[0]
    front = low.shape[0]
    clear_first(total, sums_wide, sums_inner)
    extended[:front, :] = low[...]
    extended[front : front + row_count, :] = second[...]
    fill_columns(columns, extended, masks, offsets, front, row_count)
    mixed[...] = dot(columns[...], kernel[...], NN) + inner[5:6, :]

    def make_third(rows):
        third[rows, :] = norm_silu(mixed[rows, :], inner[1:2, :], inner[3:4, :]).astype(BF16)

    by_chunks(row_count, make_third)
    grad_third[...] = dot(cotangent[...], expand[...], NT)

    def add_cotangent(rows):
        sums_wide[0] += fold_rows(cotangent[rows, :].astype(F32))

    by_chunks(row_count, add_cotangent)

    def make_grad(rows):
        grad, gain_part, shift_part = norm_silu_back(
            mixed[rows, :], inner[1:2, :], inner[3:4, :], grad_third[rows, :]
        )
        rounded = grad.astype(BF16)
        grad_mixed[rows, :] = rounded
        sums_inner[0] += fold_rows(gain_part)
        sums_inner[1] += fold_rows(shift_part)
        sums_inner[2] += fold_rows(rounded.astype(F32))

    by_chunks(row_count, make_grad)
    total[...] += dot(third[...], cotangent[...], TN)

    @at_last
    def _():
        grad_expand[...] = total[...].astype(BF16)


def routes(seq_count):
    rest = [1 << bit for bit in range(1, seq_count.bit_length() - 1)]
    return rest[::-1], rest


def pack(place, sections, keep, send):
    seq_count, fsdp_count, part = sections.seq_count, sections.fsdp_count, keep.shape[1]
    orders = routes(seq_count)
    cells = keep.shape[0] // 2

    def write(own_core):
        for shard in range(fsdp_count):
            far = place[0] ^ shard
            half = far // (fsdp_count // 2)
            within = far % (fsdp_count // 2)
            for owner in range(seq_count):
                differs = place[2] ^ owner
                spots = []
                for order in orders:
                    spot = 0
                    for bit in order:
                        spot = spot * 2 + (differs // bit) % 2
                    spots.append(spot)
                spot = jnp.where(half == 0, spots[0], spots[1])
                spot = half * cells + spot * (fsdp_count // 2) + within
                target = keep if owner % 2 == own_core else send
                filled = 0
                for start, rows, block in sections.cut(owner * part, part):
                    target[spot, filled : filled + rows, :] = block(shard, start, rows)
                    filled += rows
                if filled < part:
                    target[spot, filled:, :] = jnp.zeros((part - filled, keep.shape[2]), BF16)

    for own_core in range(2):

        @pl.when(place[2] % 2 == own_core)
        def _():
            write(own_core)


class Sections:
    def __init__(self, seq_count, fsdp_count):
        self.seq_count, self.fsdp_count = seq_count, fsdp_count
        self.entries = []

    def add(self, rows, block):
        self.entries.append((rows, block))

    def rows_of(self, total):
        part = total.shape[0] // self.fsdp_count
        self.add(
            part,
            lambda shard, start, rows: total[
                shard * part + start : shard * part + start + rows, :
            ].astype(BF16),
        )

    def kernel(self, total, taps):
        part, width = total.shape[0] // self.fsdp_count, total.shape[1] // taps
        for tap in range(taps):
            self.add(
                part,
                lambda shard, start, rows, tap=tap: total[
                    shard * part + start : shard * part + start + rows,
                    tap * width : (tap + 1) * width,
                ].astype(BF16),
            )

    def cut(self, first, rows):
        found, begin = [], 0
        for length, block in self.entries:
            low, high = max(first, begin), min(first + rows, begin + length)
            if low < high:
                found.append((low - begin, high - low, block))
            begin += length
        return found


def back_columns(offsets, front, back, grad_mixed, low, high, masks, extended, columns):
    row_count = grad_mixed.shape[0]
    if front:
        extended[:front, :] = low[...]
    extended[front : front + row_count, :] = grad_mixed[...]
    if back:
        extended[front + row_count :, :] = high[...]
    fill_columns(columns, extended, masks, offsets, front, row_count)


def hidden_grad(hidden, inner, grad_second, grad_hidden, sums_inner):
    def make_grad(rows):
        grad, gain_part, shift_part = norm_silu_back(
            hidden[rows, :], inner[0:1, :], inner[2:3, :], grad_second[rows, :]
        )
        rounded = grad.astype(BF16)
        grad_hidden[rows, :] = rounded
        sums_inner[0] += fold_rows(gain_part)
        sums_inner[1] += fold_rows(shift_part)
        sums_inner[2] += fold_rows(rounded.astype(F32))

    by_chunks(hidden.shape[0], make_grad)


def decoder_back_kernel(
    offsets,
    back,
    counts,
    place,
    grad_mixed,
    high,
    masks,
    second,
    hidden,
    first,
    flat,
    inner,
    grad_expand,
    grad_hidden,
    keep,
    send,
    sums_inner,
    extended,
    columns,
    grad_second,
    total_kernel,
    total_project,
):
    clear_first(total_kernel, total_project, sums_inner)
    back_columns(offsets, 0, back, grad_mixed, None, high, masks, extended, columns)
    grad_second[...] = dot(columns[...], flat[...], NT)
    hidden_grad(hidden, inner, grad_second, grad_hidden, sums_inner)
    total_kernel[...] += dot(second[...], columns[...], TN)
    total_project[...] += dot(first[...], grad_hidden[...], TN)

    @at_last
    def _():
        sections = Sections(*counts)
        sections.rows_of(total_project)
        sections.kernel(total_kernel, len(offsets))
        sections.kernel(grad_expand, 2)
        pack(place, sections, keep, send)


def encoder_kernel_grad_kernel(
    offsets,
    front,
    back,
    counts,
    place,
    grad_mixed,
    low,
    high,
    masks,
    second,
    grad_expand,
    keep,
    send,
    extended,
    columns,
    total_kernel,
):
    clear_first(total_kernel)
    back_columns(offsets, front, back, grad_mixed, low, high, masks, extended, columns)
    total_kernel[...] += dot(second[...], columns[...], TN)

    @at_last
    def _():
        sections = Sections(*counts)
        sections.kernel(total_kernel, len(offsets))
        sections.kernel(grad_expand, 2)
        pack(place, sections, keep, send)


def encoder_back_kernel(
    offsets,
    front,
    back,
    counts,
    place,
    grad_mixed,
    low,
    high,
    masks,
    hidden,
    first,
    flat,
    inner,
    grad_hidden,
    keep,
    send,
    sums_inner,
    extended,
    columns,
    grad_second,
    total_project,
):
    clear_first(total_project, sums_inner)
    back_columns(offsets, front, back, grad_mixed, low, high, masks, extended, columns)
    grad_second[...] = dot(columns[...], flat[...], NT)
    hidden_grad(hidden, inner, grad_second, grad_hidden, sums_inner)
    total_project[...] += dot(first[...], grad_hidden[...], TN)

    @at_last
    def _():
        sections = Sections(*counts)
        sections.rows_of(total_project)
        pack(place, sections, keep, send)


def link_back_kernel(
    grad_hidden,
    middle,
    cotangent,
    mixed,
    third,
    project,
    dec_wide,
    expand,
    enc_inner,
    grad_middle,
    grad_mixed,
    grad_expand,
    sums_wide,
    sums_inner,
    grad_first,
    branch,
    grad_third,
    total,
):
    row_count = middle.shape[0]
    clear_first(total, sums_wide, sums_inner)
    grad_first[...] = dot(grad_hidden[...], project[...], NT)

    def make_branch(rows):
        grad, gain_part, shift_part = norm_silu_back(
            middle[rows, :], dec_wide[0:1, :], dec_wide[1:2, :], grad_first[rows, :]
        )
        sums_wide[0] += fold_rows(gain_part)
        sums_wide[1] += fold_rows(shift_part)
        grad = cotangent[rows, :].astype(F32) + grad
        grad_middle[rows, :] = grad
        rounded = grad.astype(BF16)
        branch[rows, :] = rounded
        sums_wide[2] += fold_rows(rounded.astype(F32))

    by_chunks(row_count, make_branch)
    grad_third[...] = dot(branch[...], expand[...], NT)

    def make_grad(rows):
        grad, gain_part, shift_part = norm_silu_back(
            mixed[rows, :], enc_inner[1:2, :], enc_inner[3:4, :], grad_third[rows, :]
        )
        rounded = grad.astype(BF16)
        grad_mixed[rows, :] = rounded
        sums_inner[0] += fold_rows(gain_part)
        sums_inner[1] += fold_rows(shift_part)
        sums_inner[2] += fold_rows(rounded.astype(F32))

    by_chunks(row_count, make_grad)
    total[...] += dot(third[...], branch[...], TN)

    @at_last
    def _():
        grad_expand[...] = total[...].astype(BF16)


def output_kernel(third, middle, expand, wide, output, branch):
    branch[...] = dot(third[...], expand[...], NN)

    def make_output(rows):
        values = middle[rows, :] + (branch[rows, :] + wide[2:3, :])
        output[rows, :] = values.astype(BF16)

    by_chunks(middle.shape[0], make_output)


def leave_kernel(
    grad_hidden, stream, grad_middle, project, wide, grad_stream, sums_wide, grad_first
):
    row_count = stream.shape[0]
    clear_first(sums_wide)
    grad_first[...] = dot(grad_hidden[...], project[...], NT)

    def make_grad(rows):
        grad, gain_part, shift_part = norm_silu_back(
            stream[rows, :].astype(F32), wide[0:1, :], wide[1:2, :], grad_first[rows, :]
        )
        sums_wide[0] += fold_rows(gain_part)
        sums_wide[1] += fold_rows(shift_part)
        grad_stream[rows, :] = (grad_middle[rows, :] + grad).astype(BF16)

    by_chunks(row_count, make_grad)


def finish_kernel(layout, factor, place, *refs):
    count = len(refs) - len(layout) - 1
    pieces, outs, landed = refs[:count], refs[count:-1], refs[-1]
    part = landed.shape[1]
    for index, piece in enumerate(pieces):
        landed[place[2] ^ index] = piece[...]

    def write(out, where, columns, start, rows):
        done = 0
        while done < rows:
            owner, local = (start + done) // part, (start + done) % part
            size = min(rows - done, part - local)
            block = landed[owner, local : local + size, :].astype(F32) * factor
            if where is None:
                out[done : done + size, columns] = block
            else:
                out[where, done : done + size, :] = block
            done += size

    for out, (start, halves) in zip(outs, layout):
        width = landed.shape[2]
        if halves:
            for half in range(2):
                columns = slice(half * width, (half + 1) * width)
                write(out, None, columns, start + half * out.shape[0], out.shape[0])
        elif len(out.shape) == 3:
            for tap in range(out.shape[0]):
                write(out, tap, None, start + tap * out.shape[1], out.shape[1])
        else:
            write(out, None, slice(0, width), start, out.shape[0])


def stepped(array):
    rest = (0,) * (array.ndim - 1)
    return pl.BlockSpec((None,) + array.shape[1:], lambda step: (step,) + rest)


def held(array):
    zeros = (0,) * array.ndim
    return pl.BlockSpec(array.shape, lambda step: zeros, pipeline_mode=pl.Buffered(1))


def call(body, steps, moving, fixed, outs, sums, scratch, flops, loose=(), place=None, semaphores=0):
    out_shapes = [jax.ShapeDtypeStruct(shape, kind) for shape, kind in outs]
    sum_shapes = [jax.ShapeDtypeStruct(shape, kind) for shape, kind in sums]
    operands = list(moving) + list(loose) + list(fixed)
    traffic = sum(
        entry.size * entry.dtype.itemsize for entry in operands + out_shapes + sum_shapes
    )
    in_specs = [stepped(entry) for entry in moving]
    in_specs += [pl.BlockSpec(memory_space=pl.ANY) for _ in loose]
    in_specs += [held(entry) for entry in fixed]
    if place is not None:
        operands = [place] + operands
        in_specs = [pl.BlockSpec(memory_space=pltpu.SMEM)] + in_specs
    scratch_shapes = [pltpu.VMEM(shape, kind) for shape, kind in scratch]
    if semaphores:
        scratch_shapes.append(pltpu.SemaphoreType.DMA((semaphores,)))
    return pl.pallas_call(
        body,
        grid=(steps,),
        in_specs=in_specs,
        out_specs=[stepped(entry) for entry in out_shapes] + [held(entry) for entry in sum_shapes],
        out_shape=out_shapes + sum_shapes,
        scratch_shapes=scratch_shapes,
        compiler_params=pltpu.CompilerParams(
            dimension_semantics=("arbitrary",), vmem_limit_bytes=VMEM_LIMIT
        ),
        cost_estimate=pl.CostEstimate(flops=flops, bytes_accessed=traffic, transcendentals=0),
    )(*operands)


def owners(places, doc_ends):
    return jnp.sum((places[..., None] >= doc_ends[:, None, :]).astype(jnp.int32), axis=-1)


def build_masks(places, doc_ends, stream_len, offsets):
    own_doc = owners(places[None, :], doc_ends)
    columns = []
    for offset in offsets:
        partner = places + offset
        inside = (partner >= 0) & (partner < stream_len)
        columns.append(inside[None, :] & (owners(partner[None, :], doc_ends) == own_doc))
    return jnp.stack(columns, axis=-1).astype(BF16)


def to_next(block):
    count = lax.axis_size("seq")
    return lax.ppermute(block, "seq", [(i, i + 1) for i in range(count - 1)])


def to_previous(block):
    count = lax.axis_size("seq")
    return lax.ppermute(block, "seq", [(i + 1, i) for i in range(count - 1)])


def exchanged(block, axis, bit):
    return lax.ppermute(block, axis, [(i, i ^ bit) for i in range(lax.axis_size(axis))])


def round_up(value, unit):
    return -(-value // unit) * unit


def padded(block, rows):
    return jnp.pad(block, ((0, rows - block.shape[0]), (0, 0)))


class Chain:
    def __init__(self, steps):
        self.steps, self.result = steps, None
        self.pending = next(steps)

    def advance(self, arrays=None):
        try:
            self.pending = self.steps.send(self.pending if arrays is None else arrays)
        except StopIteration as stop:
            self.pending, self.result = None, stop.value
        return self

    def finish(self):
        while self.pending is not None:
            self.advance()
        return self.result


def slot(operand, *chains):
    live = [chain for chain in chains if chain.pending is not None]
    operand, arrays = lax.optimization_barrier((operand, [chain.pending for chain in live]))
    for chain, pending in zip(live, arrays):
        chain.advance(pending)
    return operand


PARTS = 4


def half_spacing(rows):
    part = round_up(rows // PARTS, 16)
    return part, (rows - part) // (PARTS - 1)


def gather_half(shard):
    part, spacing = half_spacing(shard.shape[0])
    own = lax.axis_index("seq") & (PARTS - 1)
    piece = lax.dynamic_slice_in_dim(shard, own * spacing, part, axis=0)
    (piece,) = yield [piece]
    columns = [piece]
    for bit in range(1, lax.axis_size("fsdp")):
        columns.append(exchanged(piece, "fsdp", bit))
    columns = yield columns
    others = [exchanged(entry, "seq", 2) for entry in columns]
    columns, others = yield [columns, others]
    pieces = []
    for entry, other in zip(columns, others):
        pieces += [entry, exchanged(entry, "seq", 1), other, exchanged(other, "seq", 1)]
    return pieces


def gather_full(shard):
    seq_count, fsdp_count = lax.axis_size("seq"), lax.axis_size("fsdp")
    part = round_up(shard.shape[0], 16 * seq_count) // seq_count
    piece = lax.dynamic_slice_in_dim(
        padded(shard, part * seq_count), lax.axis_index("seq") * part, part, axis=0
    )
    (piece,) = yield [piece]
    columns = [piece]
    for far in range(1, fsdp_count):
        columns.append(exchanged(piece, "fsdp", far))
    half_count = fsdp_count // 2
    halves = [[jnp.stack(columns[:half_count])], [jnp.stack(columns[half_count:])]]
    indices = [[0], [0]]
    orders = routes(seq_count)
    for step in range(len(orders[0]) + 1):
        halves = yield halves
        for half, order in enumerate(orders):
            bit = (order + [1])[step]
            halves[half] = halves[half] + [exchanged(entry, "seq", bit) for entry in halves[half]]
            indices[half] = indices[half] + [index ^ bit for index in indices[half]]
    pieces = []
    for entries, places in zip(halves, indices):
        pieces += [entry for _, entry in sorted(zip(places, entries), key=lambda pair: pair[0])]
    return pieces


def add_low(*blocks):
    total = blocks[0].astype(F32)
    for block in blocks[1:]:
        total = total + block.astype(F32)
    return total.astype(BF16)


def reduce_pieces(keep, send):
    seq_count, fsdp_count = lax.axis_size("seq"), lax.axis_size("fsdp")
    shape = (2, -1, fsdp_count // 2) + keep.shape[1:]
    (send,) = yield [send]
    parts = (keep.reshape(shape), exchanged(send, "seq", 1).reshape(shape))
    orders = routes(seq_count)
    terms = [[entry[half] for entry in parts] for half in range(2)]
    for step in range(len(orders[0])):
        size = terms[0][0].shape[0] // 2
        leaving = [add_low(*[term[size:] for term in entries]) for entries in terms]
        leaving = yield leaving
        terms = [
            [term[:size] for term in entries] + [exchanged(block, "seq", order[step])]
            for entries, block, order in zip(terms, leaving, orders)
        ]
    columns = []
    for entries in terms:
        columns += [[term[0, within] for term in entries] for within in range(fsdp_count // 2)]
    leaving = yield [add_low(*columns[far]) for far in range(1, fsdp_count)]
    arrived = [exchanged(block, "fsdp", far + 1) for far, block in enumerate(leaving)]
    pieces = [add_low(*columns[0], *arrived)]
    indices = [0]
    for bit in orders[1] + [1]:
        pieces = yield pieces
        pieces = pieces + [exchanged(piece, "seq", bit) for piece in pieces]
        indices = indices + [index ^ bit for index in indices]
    return [piece for _, piece in sorted(zip(indices, pieces), key=lambda pair: pair[0])]


def reduce_vectors(vectors):
    for axis in ("seq", "fsdp"):
        bit = 1
        while bit < lax.axis_size(axis):
            (vectors,) = yield [vectors]
            vectors = vectors + exchanged(vectors, axis, bit)
            bit *= 2
    return vectors


def local(
    characters,
    lengths,
    cotangent,
    encproject,
    enckernel,
    encexpand,
    encwidegain,
    encgains,
    encwideshift,
    encshifts,
    decproject,
    deckernel,
    decexpand,
    decwidegain,
    decgains,
    decwideshift,
    decshifts,
):
    micro, _, rows, width = characters.shape
    inner_width = encproject.shape[1]
    seq_count = lax.axis_size("seq")
    fsdp_count = lax.axis_size("fsdp")
    stream_len = rows * seq_count
    total_rows = micro * stream_len * fsdp_count
    factor = 1.0 / jnp.sqrt(jnp.float32(total_rows))
    stream = characters[:, 0]
    cot = cotangent[:, 0]

    seq_index = lax.axis_index("seq")
    place = jnp.stack([lax.axis_index("fsdp"), seq_index & (PARTS - 1), seq_index])
    place = place.astype(jnp.int32)
    def rows_of(kernel):
        return kernel.reshape(-1, kernel.shape[2])

    def halves(expand):
        return [expand[:, :inner_width], expand[:, inner_width:]]

    wide_local = [encwidegain[None], encwideshift, decwidegain[None], decwideshift]
    wide_local = jnp.concatenate(wide_local, axis=0)
    inner_local = jnp.concatenate([encgains, encshifts, decgains, decshifts], axis=0)
    vector_local = jnp.concatenate([wide_local.reshape(-1), inner_local.reshape(-1)])
    vector_shards = jnp.stack(
        [vector_local] + [exchanged(vector_local, "fsdp", far) for far in range(1, fsdp_count)]
    )
    own = lax.axis_index("fsdp")
    vector_shards = jnp.stack(
        [
            lax.dynamic_index_in_dim(vector_shards, own ^ shard, 0, keepdims=False)
            for shard in range(fsdp_count)
        ]
    ).astype(F32)

    def whole_vectors(shards, like):
        cut = shards.reshape((fsdp_count,) + like.shape)
        return jnp.transpose(cut, (1, 0, 2)).reshape(like.shape[0], -1)

    wides = whole_vectors(vector_shards[:, : wide_local.size], wide_local)
    inners = whole_vectors(vector_shards[:, wide_local.size :], inner_local)
    enc_wide, dec_wide = wides[:3], wides[3:]
    enc_inner, dec_inner = inners[:6], inners[6:]

    enc_rows = jnp.concatenate([rows_of(enckernel)] + halves(encexpand), axis=0)
    dec_rows = jnp.concatenate([decproject, rows_of(deckernel)] + halves(decexpand), axis=0)
    entry = Chain(gather_half(encproject)).advance()
    enc_gather = Chain(gather_full(enc_rows)).advance()
    dec_gather = Chain(gather_full(dec_rows)).advance()
    _, spacing = half_spacing(encproject.shape[0])

    def landing(pieces):
        count = len(pieces) * pieces[0].shape[0]
        return ((count,) + pieces[0].shape[1:], BF16), count

    places = lax.axis_index("seq") * rows + jnp.arange(rows, dtype=jnp.int32)
    doc_ends = jnp.cumsum(lengths[:, 0], axis=1)
    enc_offsets = tap_offsets(True)
    dec_offsets = tap_offsets(False)
    enc_back = [-offset for offset in enc_offsets]
    dec_back = [-offset for offset in dec_offsets]
    enc_masks = build_masks(places, doc_ends, stream_len, enc_offsets)
    dec_masks = build_masks(places, doc_ends, stream_len, dec_offsets)
    enc_back_masks = build_masks(places, doc_ends, stream_len, enc_back)
    dec_back_masks = build_masks(places, doc_ends, stream_len, dec_back)
    enc_reach = max(enc_offsets)
    dec_reach = -min(dec_offsets)

    wide_shape = (micro, rows, width)
    inner_shape = (micro, rows, inner_width)
    unit = 2 * micro * rows * width * inner_width
    tap_unit = 2 * micro * rows * inner_width * inner_width

    def enter_body(*refs):
        enter_encoder_kernel(PARTS, spacing, *refs)

    project_pieces = entry.finish()
    enc_gather.advance()
    enc_wide = slot(enc_wide, enc_gather)
    first_e, hidden_e, second_e, enc_project = call(
        enter_body,
        micro,
        [stream],
        [enc_wide, enc_inner],
        [(wide_shape, BF16), (inner_shape, F32), (inner_shape, BF16)],
        [((width, inner_width), BF16)],
        [((len(project_pieces),) + project_pieces[0].shape, BF16)],
        unit,
        project_pieces,
        place,
        len(project_pieces),
    )
    low = to_next(second_e[:, rows - enc_reach :])
    high = to_previous(second_e[:, :enc_reach])

    def middle_body(*refs):
        middle_kernel(enc_offsets, fsdp_count, *refs)

    enc_pieces = enc_gather.finish()
    dec_gather.advance()
    enc_inner = slot(enc_inner, dec_gather)
    landed, copies = landing(enc_pieces)
    mixed_e, third_e, middle, enc_expand, enc_flat = call(
        middle_body,
        micro,
        [second_e, low, high, enc_masks, stream],
        [enc_wide, enc_inner],
        [(inner_shape, F32), (inner_shape, BF16), (wide_shape, F32)],
        [((inner_width, width), BF16), ((inner_width, ENC_TAPS * inner_width), BF16)],
        [
            ((rows + 2 * enc_reach, inner_width), BF16),
            ((rows, ENC_TAPS * inner_width), BF16),
            ((ENC_TAPS * inner_width, inner_width), BF16),
            landed,
        ],
        unit + ENC_TAPS * tap_unit,
        enc_pieces,
        place,
        copies,
    )

    def enter_decoder_body(*refs):
        enter_decoder_kernel(DEC_TAPS, fsdp_count, *refs)

    dec_pieces = dec_gather.finish()
    landed, copies = landing(dec_pieces)
    first_d, hidden_d, second_d, dec_project, dec_stacked, dec_flat, dec_expand = call(
        enter_decoder_body,
        micro,
        [middle],
        [dec_wide, dec_inner],
        [(wide_shape, BF16), (inner_shape, F32), (inner_shape, BF16)],
        [
            ((width, inner_width), BF16),
            ((DEC_TAPS * inner_width, inner_width), BF16),
            ((inner_width, DEC_TAPS * inner_width), BF16),
            ((inner_width, width), BF16),
        ],
        [landed],
        unit,
        dec_pieces,
        place,
        copies,
    )
    low = to_next(second_d[:, rows - dec_reach :])

    def turn_body(*refs):
        turn_kernel(dec_offsets, *refs)

    third_d, gmixed_d, gexpand_d, turn_wide, turn_inner = call(
        turn_body,
        micro,
        [second_d, low, dec_masks, cot],
        [dec_stacked, dec_expand, dec_inner],
        [(inner_shape, BF16), (inner_shape, BF16)],
        [
            ((inner_width, width), BF16),
            ((1, 8, width), F32),
            ((3, 8, inner_width), F32),
        ],
        [
            ((rows + dec_reach, inner_width), BF16),
            ((rows, DEC_TAPS * inner_width), BF16),
            ((rows, inner_width), F32),
            ((rows, inner_width), F32),
            ((inner_width, width), F32),
        ],
        2 * unit + DEC_TAPS * tap_unit,
    )
    high = to_previous(gmixed_d[:, :dec_reach])

    counts = (seq_count, fsdp_count)

    def packed_pair(row_total):
        part = round_up(row_total, 8 * seq_count) // seq_count
        return [((seq_count * fsdp_count // 2, part, inner_width), BF16)] * 2

    shard_part = inner_width // fsdp_count

    def decoder_back_body(*refs):
        decoder_back_kernel(dec_back, dec_reach, counts, *refs)

    ghidden_d, keep_d, send_d, conv_inner_d = call(
        decoder_back_body,
        micro,
        [gmixed_d, high, dec_back_masks, second_d, hidden_d, first_d],
        [dec_flat, dec_inner, gexpand_d],
        [(inner_shape, BF16)],
        packed_pair((DEC_TAPS + 2) * shard_part + width // fsdp_count)
        + [((3, 8, inner_width), F32)],
        [
            ((rows + dec_reach, inner_width), BF16),
            ((rows, DEC_TAPS * inner_width), BF16),
            ((rows, inner_width), F32),
            ((inner_width, DEC_TAPS * inner_width), F32),
            ((width, inner_width), F32),
        ],
        unit + 2 * DEC_TAPS * tap_unit,
        place=place,
    )

    dec_reduce = Chain(reduce_pieces(keep_d, send_d))
    dec_wide = slot(dec_wide, dec_reduce)
    gmiddle, gmixed_e, gexpand_e, link_wide, link_inner = call(
        link_back_kernel,
        micro,
        [ghidden_d, middle, cot, mixed_e, third_e],
        [dec_project, dec_wide, enc_expand, enc_inner],
        [(wide_shape, F32), (inner_shape, BF16)],
        [
            ((inner_width, width), BF16),
            ((3, 8, width), F32),
            ((3, 8, inner_width), F32),
        ],
        [
            ((rows, width), F32),
            ((rows, width), BF16),
            ((rows, inner_width), F32),
            ((inner_width, width), F32),
        ],
        3 * unit,
    )
    low = to_next(gmixed_e[:, rows - enc_reach :])
    high = to_previous(gmixed_e[:, :enc_reach])
    extended_scratch = [
        ((rows + 2 * enc_reach, inner_width), BF16),
        ((rows, ENC_TAPS * inner_width), BF16),
    ]

    def kernel_grad_body(*refs):
        encoder_kernel_grad_kernel(enc_back, enc_reach, enc_reach, counts, *refs)

    gexpand_e = slot(gexpand_e, dec_reduce)
    keep_e, send_e = call(
        kernel_grad_body,
        micro,
        [gmixed_e, low, high, enc_back_masks, second_e],
        [gexpand_e],
        [],
        packed_pair((ENC_TAPS + 2) * shard_part),
        extended_scratch + [((inner_width, ENC_TAPS * inner_width), F32)],
        ENC_TAPS * tap_unit,
        place=place,
    )

    def encoder_back_body(*refs):
        encoder_back_kernel(enc_back, enc_reach, enc_reach, counts, *refs)

    enc_reduce = Chain(reduce_pieces(keep_e, send_e))
    enc_inner = slot(enc_inner, dec_reduce, enc_reduce)
    ghidden_e, keep_p, send_p, conv_inner_e = call(
        encoder_back_body,
        micro,
        [gmixed_e, low, high, enc_back_masks, hidden_e, first_e],
        [enc_flat, enc_inner],
        [(inner_shape, BF16)],
        packed_pair(width // fsdp_count) + [((3, 8, inner_width), F32)],
        extended_scratch + [((rows, inner_width), F32), ((width, inner_width), F32)],
        unit + ENC_TAPS * tap_unit,
        place=place,
    )
    entry_reduce = Chain(reduce_pieces(keep_p, send_p))
    enc_wide = slot(enc_wide, dec_reduce, enc_reduce, entry_reduce)
    gstream, leave_wide = call(
        leave_kernel,
        micro,
        [ghidden_e, stream, gmiddle],
        [enc_project, enc_wide],
        [(wide_shape, BF16)],
        [((2, 8, width), F32)],
        [((rows, width), F32)],
        unit,
    )

    sums = [leave_wide, link_wide, turn_wide, conv_inner_e, link_inner, conv_inner_d, turn_inner]
    sums = [jnp.sum(entry, axis=1).reshape(-1, inner_width) for entry in sums]
    vector_reduce = Chain(reduce_vectors(jnp.concatenate(sums, axis=0)))
    dec_wide = slot(dec_wide, dec_reduce, enc_reduce, entry_reduce, vector_reduce)
    (output,) = call(
        output_kernel,
        micro,
        [third_d, middle],
        [dec_expand, dec_wide],
        [(wide_shape, BF16)],
        [],
        [((rows, width), F32)],
        unit,
    )

    def own_columns(vectors):
        part = vectors.shape[1] // fsdp_count
        return lax.dynamic_slice_in_dim(vectors, own * part, part, axis=1)

    sums = vector_reduce.finish() * factor
    wide_sums = sums[:12].reshape(6, width)
    order = [wide_sums[:2], wide_sums[4:5], wide_sums[2:4], wide_sums[5:]]
    wide_own = own_columns(jnp.concatenate(order))
    inner_own = own_columns(sums[12:])

    def vectors(wide_rows, inner_rows):
        widegain = wide_rows[0]
        wideshift = wide_rows[1:3]
        gains = jnp.stack([inner_rows[0], inner_rows[3]])
        shifts = jnp.stack([inner_rows[1], inner_rows[4], inner_rows[2], inner_rows[5]])
        return widegain, gains, wideshift, shifts

    project_rows = width // fsdp_count
    scale = total_rows**-0.5
    shapes = {
        "project": (project_rows, inner_width),
        "expand": (shard_part, width),
    }

    def finish(chain, names):
        pieces = chain.finish()
        layout, outs, start = [], [], 0
        for name in names:
            shape = shapes.get(name, (name, shard_part, inner_width))
            layout.append((start, name == "expand"))
            outs.append(jax.ShapeDtypeStruct(shape, F32))
            size = 1
            for extent in shape:
                size *= extent
            start += size // inner_width

        def body(*refs):
            finish_kernel(layout, scale, *refs)

        whole = pl.BlockSpec(memory_space=pltpu.VMEM)
        return pl.pallas_call(
            body,
            in_specs=[pl.BlockSpec(memory_space=pltpu.SMEM)] + [whole] * len(pieces),
            out_specs=[whole] * len(outs),
            out_shape=outs,
            scratch_shapes=[pltpu.VMEM((len(pieces),) + pieces[0].shape, BF16)],
            compiler_params=pltpu.CompilerParams(vmem_limit_bytes=VMEM_LIMIT),
        )(place, *pieces)

    gproject_d, gkernel_d, gexpand_d = finish(dec_reduce, ["project", DEC_TAPS, "expand"])
    gkernel_e, gexpand_e = finish(enc_reduce, [ENC_TAPS, "expand"])
    (gproject_e,) = finish(entry_reduce, ["project"])
    return (
        output[:, None],
        gstream[:, None],
        gproject_e,
        gkernel_e,
        gexpand_e,
        *vectors(wide_own[:3], inner_own[:6]),
        gproject_d,
        gkernel_d,
        gexpand_d,
        *vectors(wide_own[3:], inner_own[6:]),
    )


def solution(mesh):
    tokens = P(None, "fsdp", "seq", None)
    weights = (
        P("fsdp", None),
        P(None, "fsdp", None),
        P("fsdp", None),
        P("fsdp"),
        P(None, "fsdp"),
        P(None, "fsdp"),
        P(None, "fsdp"),
    )
    return jax.shard_map(
        local,
        mesh=mesh,
        in_specs=(tokens, P(None, "fsdp", None), tokens) + weights + weights,
        out_specs=(tokens, tokens) + weights + weights,
        check_vma=False,
    )
```

```python
import jax
import jax.numpy as jnp
from jax import lax
from jax.experimental import pallas as pl
from jax.experimental.pallas import tpu as pltpu
from jax.sharding import PartitionSpec as P

ENC_TAPS = 5
ENC_DILATION = 8
DEC_TAPS = 3
DEC_DILATION = 16
EPSILON = 1e-05
CHUNK = 48
VMEM_LIMIT = 60 * 1024 * 1024

BF16 = jnp.bfloat16
F32 = jnp.float32
NN = (((1,), (0,)), ((), ()))
NT = (((1,), (1,)), ((), ()))
TN = (((0,), (0,)), ((), ()))


def dot(left, right, dims):
    return lax.dot_general(left, right, dims, preferred_element_type=F32)


def tap_offsets(encoder):
    if encoder:
        return [(tap - ENC_TAPS // 2) * ENC_DILATION for tap in range(ENC_TAPS)]
    return [(tap - DEC_TAPS + 1) * DEC_DILATION for tap in range(DEC_TAPS)]


def normalized(values):
    average = jnp.mean(values, axis=-1, keepdims=True)
    centred = values - average
    scale = lax.rsqrt(jnp.mean(centred * centred, axis=-1, keepdims=True) + EPSILON)
    return centred * scale, scale


def logistic(inner):
    return 0.5 * jnp.tanh(0.5 * inner) + 0.5


def norm_silu(values, gain, shift):
    unit, _ = normalized(values)
    inner = unit * gain + shift
    return inner * logistic(inner)


def norm_silu_back(values, gain, shift, grad):
    unit, scale = normalized(values)
    inner = unit * gain + shift
    gate = logistic(inner)
    grad_inner = grad * (gate + inner * gate * (1.0 - gate))
    grad_unit = grad_inner * gain
    along = jnp.mean(grad_unit * unit, axis=-1, keepdims=True)
    level = jnp.mean(grad_unit, axis=-1, keepdims=True)
    grad_values = scale * (grad_unit - level - unit * along)
    return grad_values, grad_inner * unit, grad_inner


def fold_rows(values):
    total = values[0:8]
    for start in range(8, values.shape[0], 8):
        total = total + values[start : start + 8]
    return total


def by_chunks(row_count, body):
    for start in range(0, row_count, CHUNK):
        body(pl.ds(start, CHUNK))


def clear_first(*refs):
    @pl.when(pl.program_id(0) == 0)
    def _():
        for ref in refs:
            ref[...] = jnp.zeros_like(ref)


def at_last(body):
    pl.when(pl.program_id(0) == pl.num_programs(0) - 1)(body)


def fill_columns(columns, extended, masks, offsets, front, row_count):
    width = extended.shape[-1]
    for tap, offset in enumerate(offsets):
        window = extended[front + offset : front + offset + row_count, :]
        if offset != 0:
            window = window * masks[:, tap : tap + 1]
        columns[:, tap * width : (tap + 1) * width] = window


def enter_kernel(stream, project, wide, inner, first, hidden, second):
    row_count = stream.shape[0]

    def make_first(rows):
        values = stream[rows, :].astype(F32)
        first[rows, :] = norm_silu(values, wide[0:1, :], wide[1:2, :]).astype(BF16)

    by_chunks(row_count, make_first)
    hidden[...] = dot(first[...], project[...], NN) + inner[4:5, :]

    def make_second(rows):
        second[rows, :] = norm_silu(hidden[rows, :], inner[0:1, :], inner[2:3, :]).astype(BF16)

    by_chunks(row_count, make_second)


def fetch(sources, spots, target, semaphores):
    copies = [
        pltpu.make_async_copy(source, target.at[spot], semaphores.at[index])
        for index, (source, spot) in enumerate(zip(sources, spots))
    ]
    for copy in copies:
        copy.start()
    for copy in copies:
        copy.wait()


def fetch_shards(place, own, parts, pieces, origins, landed, semaphores):
    sources, spots = [], []
    for piece, entries in zip(pieces, origins):
        for index, (far, differs) in enumerate(entries):
            sources.append(piece.at[index])
            spots.append((place[0] ^ far) * parts + (own ^ differs))
    fetch(sources, spots, landed, semaphores)


class Shards:
    def __init__(self, landed, fsdp_count):
        self.landed, self.fsdp_count = landed, fsdp_count
        self.seq_count = landed.shape[0] // fsdp_count

    def spread(self, shard, start, rows, write):
        part, done = self.landed.shape[1], 0
        while done < rows:
            owner, local = (start + done) // part, (start + done) % part
            size = min(rows - done, part - local)
            write(done, self.landed[shard * self.seq_count + owner, local : local + size, :])
            done += size


def enter_encoder_kernel(origins, spacing, place, stream, *refs):
    pieces, refs = refs[:-8], refs[-8:]
    wide, inner, first, hidden, second, project, landed, semaphores = refs

    @pl.when(pl.program_id(0) == 0)
    def _():
        fetch_shards(place, place[1], PARTS, pieces, origins, landed, semaphores)
        shard_rows = project.shape[0] * PARTS // landed.shape[0]
        part = shard_rows - (PARTS - 1) * spacing
        for index in range(landed.shape[0]):
            start = index // PARTS * shard_rows + index % PARTS * spacing
            project[start : start + part, :] = landed[index, :part, :]

    enter_kernel(stream, project, wide, inner, first, hidden, second)


def unpack_kernel(shards, start, taps, kernel, flat):
    width = flat.shape[0]
    part = width // shards.fsdp_count
    for own in range(shards.fsdp_count):
        for tap in range(taps):

            def write(done, block):
                row = own * part + done
                size = block.shape[0]
                kernel[tap * width + row : tap * width + row + size, :] = block
                flat[row : row + size, tap * width : (tap + 1) * width] = block

            shards.spread(own, start + tap * part, part, write)


def unpack_expand(shards, start, expand):
    width = expand.shape[1] // 2
    part = expand.shape[0] // shards.fsdp_count
    for own in range(shards.fsdp_count):
        for half in range(2):

            def write(done, block):
                row = own * part + done
                expand[row : row + block.shape[0], half * width : (half + 1) * width] = block

            shards.spread(own, start + half * part, part, write)


def unpack_rows(shards, start, whole):
    part = whole.shape[0] // shards.fsdp_count
    for own in range(shards.fsdp_count):

        def write(done, block):
            row = own * part + done
            whole[row : row + block.shape[0], :] = block

        shards.spread(own, start, part, write)


def middle_kernel(offsets, counts, origins, place, second_in, low, high, masks, stream, *refs):
    pieces, refs = refs[:-13], refs[-13:]
    enc_wide, enc_inner, mixed, third, middle, expand, flat, project = refs[:8]
    extended, columns, kernel, landed, semaphores = refs[8:]
    row_count = stream.shape[0]
    front = low.shape[0]

    @pl.when(pl.program_id(0) == 0)
    def _():
        seq_count, fsdp_count = counts
        fetch_shards(place, place[2], seq_count, pieces, origins, landed, semaphores)
        shards = Shards(landed, fsdp_count)
        unpack_kernel(shards, 0, len(offsets), kernel, flat)
        start = kernel.shape[0] // fsdp_count
        unpack_expand(shards, start, expand)
        unpack_rows(shards, start + expand.shape[0] * 2 // fsdp_count, project)

    extended[:front, :] = low[...]
    extended[front : front + row_count, :] = second_in[...]
    extended[front + row_count :, :] = high[...]
    fill_columns(columns, extended, masks, offsets, front, row_count)
    mixed[...] = dot(columns[...], kernel[...], NN) + enc_inner[5:6, :]

    def make_third(rows):
        third[rows, :] = norm_silu(mixed[rows, :], enc_inner[1:2, :], enc_inner[3:4, :]).astype(
            BF16
        )

    by_chunks(row_count, make_third)
    middle[...] = dot(third[...], expand[...], NN)

    def make_middle(rows):
        branch = middle[rows, :] + enc_wide[2:3, :]
        middle[rows, :] = stream[rows, :].astype(F32) + branch

    by_chunks(row_count, make_middle)


def turn_kernel(offsets, counts, origins, place, second, low, masks, cotangent, *refs):
    pieces, refs = refs[:-16], refs[-16:]
    inner, third, grad_mixed, grad_expand, flat, expand, sums_wide, sums_inner = refs[:8]
    extended, columns, mixed, grad_third, total, kernel, landed, semaphores = refs[8:]
    row_count = cotangent.shape[0]
    front = low.shape[0]
    clear_first(total, sums_wide, sums_inner)

    @pl.when(pl.program_id(0) == 0)
    def _():
        seq_count, fsdp_count = counts
        fetch_shards(place, place[2], seq_count, pieces, origins, landed, semaphores)
        shards = Shards(landed, fsdp_count)
        unpack_kernel(shards, 0, len(offsets), kernel, flat)
        unpack_expand(shards, kernel.shape[0] // fsdp_count, expand)

    extended[:front, :] = low[...]
    extended[front : front + row_count, :] = second[...]
    fill_columns(columns, extended, masks, offsets, front, row_count)
    mixed[...] = dot(columns[...], kernel[...], NN) + inner[5:6, :]

    def make_third(rows):
        third[rows, :] = norm_silu(mixed[rows, :], inner[1:2, :], inner[3:4, :]).astype(BF16)

    by_chunks(row_count, make_third)
    grad_third[...] = dot(cotangent[...], expand[...], NT)

    def add_cotangent(rows):
        sums_wide[0] += fold_rows(cotangent[rows, :].astype(F32))

    by_chunks(row_count, add_cotangent)

    def make_grad(rows):
        grad, gain_part, shift_part = norm_silu_back(
            mixed[rows, :], inner[1:2, :], inner[3:4, :], grad_third[rows, :]
        )
        rounded = grad.astype(BF16)
        grad_mixed[rows, :] = rounded
        sums_inner[0] += fold_rows(gain_part)
        sums_inner[1] += fold_rows(shift_part)
        sums_inner[2] += fold_rows(rounded.astype(F32))

    by_chunks(row_count, make_grad)
    total[...] += dot(third[...], cotangent[...], TN)

    @at_last
    def _():
        grad_expand[...] = total[...].astype(BF16)


def routes(seq_count):
    rest = [1 << bit for bit in range(1, seq_count.bit_length() - 1)]
    return rest[::-1], rest


def pack(place, sections, keep, send):
    seq_count, fsdp_count, part = sections.seq_count, sections.fsdp_count, keep.shape[1]
    orders = routes(seq_count)
    cells = keep.shape[0] // 2

    def write(own_core):
        for shard in range(fsdp_count):
            far = place[0] ^ shard
            half = far // (fsdp_count // 2)
            within = far % (fsdp_count // 2)
            for owner in range(seq_count):
                differs = place[2] ^ owner
                spots = []
                for order in orders:
                    spot = 0
                    for bit in order:
                        spot = spot * 2 + (differs // bit) % 2
                    spots.append(spot)
                spot = jnp.where(half == 0, spots[0], spots[1])
                spot = half * cells + spot * (fsdp_count // 2) + within
                target = keep if owner % 2 == own_core else send
                filled = 0
                for start, rows, block in sections.cut(owner * part, part):
                    target[spot, filled : filled + rows, :] = block(shard, start, rows)
                    filled += rows
                if filled < part:
                    target[spot, filled:, :] = jnp.zeros((part - filled, keep.shape[2]), BF16)

    for own_core in range(2):

        @pl.when(place[2] % 2 == own_core)
        def _():
            write(own_core)


class Sections:
    def __init__(self, seq_count, fsdp_count):
        self.seq_count, self.fsdp_count = seq_count, fsdp_count
        self.entries = []

    def add(self, rows, block):
        self.entries.append((rows, block))

    def rows_of(self, total):
        part = total.shape[0] // self.fsdp_count
        self.add(
            part,
            lambda shard, start, rows: total[
                shard * part + start : shard * part + start + rows, :
            ].astype(BF16),
        )

    def kernel(self, total, taps):
        part, width = total.shape[0] // self.fsdp_count, total.shape[1] // taps
        for tap in range(taps):
            self.add(
                part,
                lambda shard, start, rows, tap=tap: total[
                    shard * part + start : shard * part + start + rows,
                    tap * width : (tap + 1) * width,
                ].astype(BF16),
            )

    def cut(self, first, rows):
        found, begin = [], 0
        for length, block in self.entries:
            low, high = max(first, begin), min(first + rows, begin + length)
            if low < high:
                found.append((low - begin, high - low, block))
            begin += length
        return found


def back_columns(offsets, front, back, grad_mixed, low, high, masks, extended, columns):
    row_count = grad_mixed.shape[0]
    if front:
        extended[:front, :] = low[...]
    extended[front : front + row_count, :] = grad_mixed[...]
    if back:
        extended[front + row_count :, :] = high[...]
    fill_columns(columns, extended, masks, offsets, front, row_count)


def hidden_grad(hidden, inner, grad_second, grad_hidden, sums_inner):
    def make_grad(rows):
        grad, gain_part, shift_part = norm_silu_back(
            hidden[rows, :], inner[0:1, :], inner[2:3, :], grad_second[rows, :]
        )
        rounded = grad.astype(BF16)
        grad_hidden[rows, :] = rounded
        sums_inner[0] += fold_rows(gain_part)
        sums_inner[1] += fold_rows(shift_part)
        sums_inner[2] += fold_rows(rounded.astype(F32))

    by_chunks(hidden.shape[0], make_grad)


def decoder_back_kernel(
    offsets,
    back,
    counts,
    place,
    grad_mixed,
    high,
    masks,
    second,
    hidden,
    first,
    flat,
    inner,
    grad_expand,
    grad_hidden,
    keep,
    send,
    sums_inner,
    extended,
    columns,
    grad_second,
    total_kernel,
    total_project,
):
    clear_first(total_kernel, total_project, sums_inner)
    back_columns(offsets, 0, back, grad_mixed, None, high, masks, extended, columns)
    grad_second[...] = dot(columns[...], flat[...], NT)
    hidden_grad(hidden, inner, grad_second, grad_hidden, sums_inner)
    total_kernel[...] += dot(second[...], columns[...], TN)
    total_project[...] += dot(first[...], grad_hidden[...], TN)

    @at_last
    def _():
        sections = Sections(*counts)
        sections.rows_of(total_project)
        sections.kernel(total_kernel, len(offsets))
        sections.kernel(grad_expand, 2)
        pack(place, sections, keep, send)


def encoder_kernel_grad_kernel(
    offsets,
    front,
    back,
    counts,
    place,
    grad_mixed,
    low,
    high,
    masks,
    second,
    grad_expand,
    keep,
    send,
    extended,
    columns,
    total_kernel,
):
    clear_first(total_kernel)
    back_columns(offsets, front, back, grad_mixed, low, high, masks, extended, columns)
    total_kernel[...] += dot(second[...], columns[...], TN)

    @at_last
    def _():
        sections = Sections(*counts)
        sections.kernel(total_kernel, len(offsets))
        sections.kernel(grad_expand, 2)
        pack(place, sections, keep, send)


def encoder_back_kernel(
    offsets,
    front,
    back,
    grad_mixed,
    low,
    high,
    masks,
    hidden,
    flat,
    inner,
    grad_hidden,
    sums_inner,
    extended,
    columns,
    grad_second,
):
    clear_first(sums_inner)
    back_columns(offsets, front, back, grad_mixed, low, high, masks, extended, columns)
    grad_second[...] = dot(columns[...], flat[...], NT)
    hidden_grad(hidden, inner, grad_second, grad_hidden, sums_inner)


def project_grad_kernel(counts, place, first, grad_hidden, keep, send, total):
    clear_first(total)
    total[...] += dot(first[...], grad_hidden[...], TN)

    @at_last
    def _():
        sections = Sections(*counts)
        sections.rows_of(total)
        pack(place, sections, keep, send)


def link_back_kernel(
    grad_hidden,
    middle,
    cotangent,
    mixed,
    third,
    project,
    dec_wide,
    expand,
    enc_inner,
    grad_middle,
    grad_mixed,
    grad_expand,
    sums_wide,
    sums_inner,
    grad_first,
    branch,
    grad_third,
    total,
):
    row_count = middle.shape[0]
    clear_first(total, sums_wide, sums_inner)
    grad_first[...] = dot(grad_hidden[...], project[...], NT)

    def make_branch(rows):
        grad, gain_part, shift_part = norm_silu_back(
            middle[rows, :], dec_wide[0:1, :], dec_wide[1:2, :], grad_first[rows, :]
        )
        sums_wide[0] += fold_rows(gain_part)
        sums_wide[1] += fold_rows(shift_part)
        grad = cotangent[rows, :].astype(F32) + grad
        grad_middle[rows, :] = grad
        rounded = grad.astype(BF16)
        branch[rows, :] = rounded
        sums_wide[2] += fold_rows(rounded.astype(F32))

    by_chunks(row_count, make_branch)
    grad_third[...] = dot(branch[...], expand[...], NT)

    def make_grad(rows):
        grad, gain_part, shift_part = norm_silu_back(
            mixed[rows, :], enc_inner[1:2, :], enc_inner[3:4, :], grad_third[rows, :]
        )
        rounded = grad.astype(BF16)
        grad_mixed[rows, :] = rounded
        sums_inner[0] += fold_rows(gain_part)
        sums_inner[1] += fold_rows(shift_part)
        sums_inner[2] += fold_rows(rounded.astype(F32))

    by_chunks(row_count, make_grad)
    total[...] += dot(third[...], branch[...], TN)

    @at_last
    def _():
        grad_expand[...] = total[...].astype(BF16)


def output_kernel(third, middle, expand, wide, output, branch):
    branch[...] = dot(third[...], expand[...], NN)

    def make_output(rows):
        values = middle[rows, :] + (branch[rows, :] + wide[2:3, :])
        output[rows, :] = values.astype(BF16)

    by_chunks(middle.shape[0], make_output)


def leave_kernel(
    grad_hidden, stream, grad_middle, project, wide, grad_stream, sums_wide, grad_first
):
    row_count = stream.shape[0]
    clear_first(sums_wide)
    grad_first[...] = dot(grad_hidden[...], project[...], NT)

    def make_grad(rows):
        grad, gain_part, shift_part = norm_silu_back(
            stream[rows, :].astype(F32), wide[0:1, :], wide[1:2, :], grad_first[rows, :]
        )
        sums_wide[0] += fold_rows(gain_part)
        sums_wide[1] += fold_rows(shift_part)
        grad_stream[rows, :] = (grad_middle[rows, :] + grad).astype(BF16)

    by_chunks(row_count, make_grad)


def finish_kernel(layout, factor, indices, place, *refs):
    count = len(indices)
    pieces, outs, landed = refs[:count], refs[count:-1], refs[-1]
    part = landed.shape[1]
    for piece, entries in zip(pieces, indices):
        for spot, index in enumerate(entries):
            landed[place[2] ^ index] = piece[spot]

    def write(out, where, columns, start, rows):
        done = 0
        while done < rows:
            owner, local = (start + done) // part, (start + done) % part
            size = min(rows - done, part - local)
            block = landed[owner, local : local + size, :].astype(F32) * factor
            if where is None:
                out[done : done + size, columns] = block
            else:
                out[where, done : done + size, :] = block
            done += size

    for out, (start, halves) in zip(outs, layout):
        width = landed.shape[2]
        if halves:
            for half in range(2):
                columns = slice(half * width, (half + 1) * width)
                write(out, None, columns, start + half * out.shape[0], out.shape[0])
        elif len(out.shape) == 3:
            for tap in range(out.shape[0]):
                write(out, tap, None, start + tap * out.shape[1], out.shape[1])
        else:
            write(out, None, slice(0, width), start, out.shape[0])


def stepped(array, offset):
    rest = (0,) * (array.ndim - 1)
    return pl.BlockSpec((None,) + array.shape[1:], lambda step: (step + offset,) + rest)


def held(array):
    zeros = (0,) * array.ndim
    return pl.BlockSpec(array.shape, lambda step: zeros, pipeline_mode=pl.Buffered(1))


def call(
    body,
    steps,
    moving,
    fixed,
    outs,
    sums,
    scratch,
    flops,
    loose=(),
    place=None,
    semaphores=0,
    offset=0,
    carried=(),
):
    out_shapes = [jax.ShapeDtypeStruct(shape, kind) for shape, kind in outs]
    sum_shapes = [jax.ShapeDtypeStruct(shape, kind) for shape, kind in sums]
    operands = list(moving) + list(loose) + list(fixed)
    traffic = sum(
        entry.size * entry.dtype.itemsize for entry in operands + out_shapes + sum_shapes
    )
    in_specs = [stepped(entry, offset) for entry in moving]
    in_specs += [pl.BlockSpec(memory_space=pl.ANY) for _ in loose]
    in_specs += [held(entry) for entry in fixed]
    if place is not None:
        operands = [place] + operands
        in_specs = [pl.BlockSpec(memory_space=pltpu.SMEM)] + in_specs
    count = len(operands)
    operands += list(carried)
    in_specs += [pl.BlockSpec(memory_space=pl.ANY) for _ in carried]
    scratch_shapes = [pltpu.VMEM(shape, kind) for shape, kind in scratch]
    if semaphores:
        scratch_shapes.append(pltpu.SemaphoreType.DMA((semaphores,)))

    def kernel(*refs):
        body(*refs[:count], *refs[count + len(carried) :])

    return pl.pallas_call(
        kernel,
        grid=(steps,),
        in_specs=in_specs,
        out_specs=[stepped(entry, offset) for entry in out_shapes]
        + [held(entry) for entry in sum_shapes],
        out_shape=out_shapes + sum_shapes,
        scratch_shapes=scratch_shapes,
        input_output_aliases={count + index: index for index in range(len(carried))},
        compiler_params=pltpu.CompilerParams(
            dimension_semantics=("arbitrary",), vmem_limit_bytes=VMEM_LIMIT
        ),
        cost_estimate=pl.CostEstimate(flops=flops, bytes_accessed=traffic, transcendentals=0),
    )(*operands)


def owners(places, doc_ends):
    return jnp.sum((places[..., None] >= doc_ends[:, None, :]).astype(jnp.int32), axis=-1)


def build_masks(places, doc_ends, stream_len, offsets):
    own_doc = owners(places[None, :], doc_ends)
    columns = []
    for offset in offsets:
        partner = places + offset
        inside = (partner >= 0) & (partner < stream_len)
        columns.append(inside[None, :] & (owners(partner[None, :], doc_ends) == own_doc))
    return jnp.stack(columns, axis=-1).astype(BF16)


def to_next(block):
    count = lax.axis_size("seq")
    return lax.ppermute(block, "seq", [(i, i + 1) for i in range(count - 1)])


def to_previous(block):
    count = lax.axis_size("seq")
    return lax.ppermute(block, "seq", [(i + 1, i) for i in range(count - 1)])


def exchanged(block, axis, bit):
    return lax.ppermute(block, axis, [(i, i ^ bit) for i in range(lax.axis_size(axis))])


def round_up(value, unit):
    return -(-value // unit) * unit


def padded(block, rows):
    return jnp.pad(block, ((0, rows - block.shape[0]), (0, 0)))


class Chain:
    def __init__(self, steps):
        self.steps, self.result = steps, None
        self.pending = next(steps)

    def advance(self, arrays=None):
        try:
            self.pending = self.steps.send(self.pending if arrays is None else arrays)
        except StopIteration as stop:
            self.pending, self.result = None, stop.value
        return self

    def finish(self):
        while self.pending is not None:
            self.advance()
        return self.result


def slot(operand, *chains):
    live = [chain for chain in chains if chain.pending is not None]
    operand, arrays = lax.optimization_barrier((operand, [chain.pending for chain in live]))
    for chain, pending in zip(live, arrays):
        chain.advance(pending)
    return operand


PARTS = 4


def half_spacing(rows):
    part = round_up(rows // PARTS, 16)
    return part, (rows - part) // (PARTS - 1)


def tiled(block):
    return block.reshape(block.shape[0] // 8, 8, block.shape[1])


class Spread:
    def __init__(self, columns, fars, bits):
        self.parts = [jnp.stack(columns)]
        self.bits, self.step = bits, 0
        self.origins = [(far, 0) for far in fars]
        self.arrays, self.all_origins = [], []

    def moved(self, entries, bit):
        return [(far, differs ^ bit) for far, differs in entries]

    def advance(self, block):
        bit = self.bits[self.step]
        other = exchanged(block, "seq", bit)
        more = self.moved(self.origins, bit)
        self.step += 1
        if self.step < len(self.bits):
            self.parts = [block, other]
            self.origins = self.origins + more
        else:
            self.arrays = [other, block, exchanged(block, "seq", 1)]
            self.all_origins = [more, self.origins, self.moved(self.origins, 1)]

    def cross(self, arrays):
        self.arrays = arrays + [exchanged(arrays[0], "seq", 1)]
        self.all_origins.append(self.moved(self.all_origins[0], 1))


def move(spreads, crossing, before=(), after=()):
    parts, arrays, after = lax.optimization_barrier(
        ([entry.parts for entry in spreads], [entry.arrays for entry in crossing], after)
    )
    blocks = [jnp.concatenate(pair, axis=0) if len(pair) > 1 else pair[0] for pair in parts]
    blocks, arrays, before = lax.optimization_barrier((blocks, arrays, before))
    for entry, block in zip(spreads, blocks):
        entry.advance(block)
    for entry, own in zip(crossing, arrays):
        entry.cross(own)
    return tuple(before) + tuple(after)


def in_progress(spreads):
    return spreads[0].step < len(spreads[0].bits) - 1


def received(spreads):
    arrays = [
        array.reshape(array.shape[0], -1, array.shape[-1])
        for entry in spreads
        for array in entry.arrays
    ]
    origins = [entries for entry in spreads for entries in entry.all_origins]
    return arrays, origins


def along_fsdp(block, fars=None):
    fars = range(1, lax.axis_size("fsdp")) if fars is None else fars
    return [block] + [exchanged(block, "fsdp", far) for far in fars]


def spread_pair(columns):
    orders = routes(lax.axis_size("seq"))
    middle = len(columns) // 2
    return [
        Spread(columns[:middle], range(middle), orders[0]),
        Spread(columns[middle:], range(middle, len(columns)), orders[1]),
    ]


def half_piece(shard):
    part, spacing = half_spacing(shard.shape[0])
    own = lax.axis_index("seq") & (PARTS - 1)
    return lax.dynamic_slice_in_dim(shard, own * spacing, part, axis=0)


def full_piece(shard):
    seq_count = lax.axis_size("seq")
    part = round_up(shard.shape[0], 8 * seq_count) // seq_count
    return tiled(
        lax.dynamic_slice_in_dim(
            padded(shard, part * seq_count), lax.axis_index("seq") * part, part, axis=0
        )
    )


def add_low(*blocks):
    total = blocks[0].astype(F32)
    for block in blocks[1:]:
        total = total + block.astype(F32)
    return total.astype(BF16)


def reduce_pieces(keep, send):
    seq_count, fsdp_count = lax.axis_size("seq"), lax.axis_size("fsdp")
    shape = (2, -1, fsdp_count // 2) + keep.shape[1:]
    (send,) = yield [send]
    parts = (keep.reshape(shape), exchanged(send, "seq", 1).reshape(shape))
    orders = routes(seq_count)
    terms = [[entry[half] for entry in parts] for half in range(2)]
    for step in range(len(orders[0])):
        size = terms[0][0].shape[0] // 2
        leaving = [add_low(*[term[size:] for term in entries]) for entries in terms]
        leaving = yield leaving
        terms = [
            [term[:size] for term in entries] + [exchanged(block, "seq", order[step])]
            for entries, block, order in zip(terms, leaving, orders)
        ]
    columns = []
    for entries in terms:
        columns += [[term[0, within] for term in entries] for within in range(fsdp_count // 2)]
    leaving = yield [add_low(*columns[far]) for far in range(1, fsdp_count)]
    arrived = [exchanged(block, "fsdp", far + 1) for far, block in enumerate(leaving)]
    block, indices = add_low(*columns[0], *arrived)[None], [0]
    for bit in orders[1]:
        (block,) = yield [block]
        block = jnp.concatenate([block, exchanged(block, "seq", bit)], axis=0)
        indices = indices + [index ^ bit for index in indices]
    (block,) = yield [block]
    return [block, exchanged(block, "seq", 1)], [indices, [index ^ 1 for index in indices]]


def reduce_vectors(vectors):
    for axis in ("seq", "fsdp"):
        bit = 1
        while bit < lax.axis_size(axis):
            (vectors,) = yield [vectors]
            vectors = vectors + exchanged(vectors, axis, bit)
            bit *= 2
    return vectors


def local(
    characters,
    lengths,
    cotangent,
    encproject,
    enckernel,
    encexpand,
    encwidegain,
    encgains,
    encwideshift,
    encshifts,
    decproject,
    deckernel,
    decexpand,
    decwidegain,
    decgains,
    decwideshift,
    decshifts,
):
    micro, _, rows, width = characters.shape
    inner_width = encproject.shape[1]
    seq_count = lax.axis_size("seq")
    fsdp_count = lax.axis_size("fsdp")
    stream_len = rows * seq_count
    total_rows = micro * stream_len * fsdp_count
    factor = 1.0 / jnp.sqrt(jnp.float32(total_rows))
    stream = characters[:, 0]
    cot = cotangent[:, 0]

    seq_index = lax.axis_index("seq")
    place = jnp.stack([lax.axis_index("fsdp"), seq_index & (PARTS - 1), seq_index])
    place = place.astype(jnp.int32)
    def rows_of(kernel):
        return kernel.reshape(-1, kernel.shape[2])

    def halves(expand):
        return [expand[:, :inner_width], expand[:, inner_width:]]

    wide_local = [encwidegain[None], encwideshift, decwidegain[None], decwideshift]
    wide_local = jnp.concatenate(wide_local, axis=0)
    inner_local = jnp.concatenate([encgains, encshifts, decgains, decshifts], axis=0)
    vector_local = jnp.concatenate([wide_local.reshape(-1), inner_local.reshape(-1)])
    enc_rows = jnp.concatenate([rows_of(enckernel)] + halves(encexpand) + [decproject], axis=0)
    dec_rows = jnp.concatenate([rows_of(deckernel)] + halves(decexpand), axis=0)
    _, spacing = half_spacing(encproject.shape[0])
    counts = (seq_count, fsdp_count)
    enc_own, dec_own = full_piece(enc_rows), full_piece(dec_rows)
    vector_rows = round_up(vector_local.size, 8 * inner_width) // inner_width
    vector_piece = jnp.pad(vector_local, (0, vector_rows * inner_width - vector_local.size))
    vector_piece = vector_piece.reshape(vector_rows, inner_width)
    entry_piece = jnp.concatenate([half_piece(encproject), vector_piece], axis=0)
    entry_columns = along_fsdp(tiled(entry_piece))
    entry_spread = Spread(entry_columns, range(fsdp_count), [2])
    (enc_own,) = move([entry_spread], [], (enc_own,))
    enc_spreads = spread_pair(along_fsdp(enc_own))
    vector_shards = jnp.stack(
        [column[-vector_rows // 8 :].reshape(-1)[: vector_local.size] for column in entry_columns]
    )
    own = lax.axis_index("fsdp")
    vector_shards = jnp.stack(
        [
            lax.dynamic_index_in_dim(vector_shards, own ^ shard, 0, keepdims=False)
            for shard in range(fsdp_count)
        ]
    ).astype(F32)

    def whole_vectors(shards, like):
        cut = shards.reshape((fsdp_count,) + like.shape)
        return jnp.transpose(cut, (1, 0, 2)).reshape(like.shape[0], -1)

    wides = whole_vectors(vector_shards[:, : wide_local.size], wide_local)
    inners = whole_vectors(vector_shards[:, wide_local.size :], inner_local)
    enc_wide, dec_wide = wides[:3], wides[3:]
    enc_inner, dec_inner = inners[:6], inners[6:]

    far_half = fsdp_count // 2 + 1
    (dec_own,) = move(enc_spreads, [entry_spread], (dec_own,))
    dec_columns = along_fsdp(dec_own, range(1, far_half))
    project_pieces, entry_origins = received([entry_spread])
    while in_progress(enc_spreads):
        move(enc_spreads, [])

    def landing(pieces):
        count = sum(piece.shape[0] for piece in pieces)
        return ((count,) + pieces[0].shape[1:], BF16), count

    places = lax.axis_index("seq") * rows + jnp.arange(rows, dtype=jnp.int32)
    doc_ends = jnp.cumsum(lengths[:, 0], axis=1)
    enc_offsets = tap_offsets(True)
    dec_offsets = tap_offsets(False)
    enc_back = [-offset for offset in enc_offsets]
    dec_back = [-offset for offset in dec_offsets]
    enc_masks = build_masks(places, doc_ends, stream_len, enc_offsets)
    dec_masks = build_masks(places, doc_ends, stream_len, dec_offsets)
    enc_back_masks = build_masks(places, doc_ends, stream_len, enc_back)
    dec_back_masks = build_masks(places, doc_ends, stream_len, dec_back)
    enc_reach = max(enc_offsets)
    dec_reach = -min(dec_offsets)

    wide_shape = (micro, rows, width)
    inner_shape = (micro, rows, inner_width)
    unit = 2 * micro * rows * width * inner_width
    tap_unit = 2 * micro * rows * inner_width * inner_width

    def enter_body(*refs):
        enter_encoder_kernel(entry_origins, spacing, *refs)

    landed, copies = landing(project_pieces)
    enc_wide, dec_columns = move(enc_spreads, [], (enc_wide, dec_columns))
    dec_columns += along_fsdp(dec_columns[0], range(far_half, fsdp_count))[1:]
    dec_spreads = spread_pair(dec_columns)
    entered_shapes = [(wide_shape, BF16), (inner_shape, F32), (inner_shape, BF16)]
    first_e, hidden_e, second_e, enc_project = call(
        enter_body,
        micro,
        [stream],
        [enc_wide, enc_inner],
        entered_shapes,
        [((width, inner_width), BF16)],
        [landed],
        unit,
        project_pieces,
        place,
        copies,
    )
    tail, head = second_e[:, rows - enc_reach :], second_e[:, :enc_reach]
    while dec_spreads[0].step < len(dec_spreads[0].bits) - 2:
        move(dec_spreads, [])
    tail, head = move(dec_spreads, enc_spreads, after=(tail, head))
    low, high = to_next(tail), to_previous(head)
    enc_pieces, enc_origins = received(enc_spreads)

    def middle_body(*refs):
        middle_kernel(enc_offsets, counts, enc_origins, *refs)

    landed, copies = landing(enc_pieces)
    mixed_e, third_e, middle, enc_expand, enc_flat, dec_project = call(
        middle_body,
        micro,
        [second_e, low, high, enc_masks, stream],
        [enc_wide, enc_inner],
        [(inner_shape, F32), (inner_shape, BF16), (wide_shape, F32)],
        [
            ((inner_width, width), BF16),
            ((inner_width, ENC_TAPS * inner_width), BF16),
            ((width, inner_width), BF16),
        ],
        [
            ((rows + 2 * enc_reach, inner_width), BF16),
            ((rows, ENC_TAPS * inner_width), BF16),
            ((ENC_TAPS * inner_width, inner_width), BF16),
            landed,
        ],
        unit + ENC_TAPS * tap_unit,
        enc_pieces,
        place,
        copies,
    )

    def enter_decoder_body(stream_in, wide, inner, project, *refs):
        enter_kernel(stream_in, project, wide, inner, *refs)

    dec_inner, enc_expand = move(dec_spreads, [], (dec_inner,), (enc_expand,))
    first_d, hidden_d, second_d = call(
        enter_decoder_body,
        micro,
        [middle],
        [dec_wide, dec_inner, dec_project],
        [(wide_shape, BF16), (inner_shape, F32), (inner_shape, BF16)],
        [],
        [],
        unit,
    )
    (tail,) = move([], dec_spreads, after=(second_d[:, rows - dec_reach :],))
    dec_pieces, dec_origins = received(dec_spreads)
    low = to_next(tail)

    def turn_body(*refs):
        turn_kernel(dec_offsets, counts, dec_origins, *refs)

    landed, copies = landing(dec_pieces)
    third_d, gmixed_d, gexpand_d, dec_flat, dec_expand, turn_wide, turn_inner = call(
        turn_body,
        micro,
        [second_d, low, dec_masks, cot],
        [dec_inner],
        [(inner_shape, BF16), (inner_shape, BF16)],
        [
            ((inner_width, width), BF16),
            ((inner_width, DEC_TAPS * inner_width), BF16),
            ((inner_width, width), BF16),
            ((1, 8, width), F32),
            ((3, 8, inner_width), F32),
        ],
        [
            ((rows + dec_reach, inner_width), BF16),
            ((rows, DEC_TAPS * inner_width), BF16),
            ((rows, inner_width), F32),
            ((rows, inner_width), F32),
            ((inner_width, width), F32),
            ((DEC_TAPS * inner_width, inner_width), BF16),
            landed,
        ],
        2 * unit + DEC_TAPS * tap_unit,
        dec_pieces,
        place,
        copies,
    )
    high = to_previous(gmixed_d[:, :dec_reach])

    def packed_pair(row_total):
        part = round_up(row_total, 8 * seq_count) // seq_count
        return [((seq_count * fsdp_count // 2, part, inner_width), BF16)] * 2

    shard_part = inner_width // fsdp_count

    def decoder_back_body(*refs):
        decoder_back_kernel(dec_back, dec_reach, counts, *refs)

    ghidden_d, keep_d, send_d, conv_inner_d = call(
        decoder_back_body,
        micro,
        [gmixed_d, high, dec_back_masks, second_d, hidden_d, first_d],
        [dec_flat, dec_inner, gexpand_d],
        [(inner_shape, BF16)],
        packed_pair((DEC_TAPS + 2) * shard_part + width // fsdp_count)
        + [((3, 8, inner_width), F32)],
        [
            ((rows + dec_reach, inner_width), BF16),
            ((rows, DEC_TAPS * inner_width), BF16),
            ((rows, inner_width), F32),
            ((inner_width, DEC_TAPS * inner_width), F32),
            ((width, inner_width), F32),
        ],
        unit + 2 * DEC_TAPS * tap_unit,
        place=place,
    )

    dec_reduce = Chain(reduce_pieces(keep_d, send_d))
    dec_wide = slot(dec_wide, dec_reduce)
    gmiddle, gmixed_e, gexpand_e, link_wide, link_inner = call(
        link_back_kernel,
        micro,
        [ghidden_d, middle, cot, mixed_e, third_e],
        [dec_project, dec_wide, enc_expand, enc_inner],
        [(wide_shape, F32), (inner_shape, BF16)],
        [
            ((inner_width, width), BF16),
            ((3, 8, width), F32),
            ((3, 8, inner_width), F32),
        ],
        [
            ((rows, width), F32),
            ((rows, width), BF16),
            ((rows, inner_width), F32),
            ((inner_width, width), F32),
        ],
        3 * unit,
    )
    low = to_next(gmixed_e[:, rows - enc_reach :])
    high = to_previous(gmixed_e[:, :enc_reach])
    extended_scratch = [
        ((rows + 2 * enc_reach, inner_width), BF16),
        ((rows, ENC_TAPS * inner_width), BF16),
    ]

    def kernel_grad_body(*refs):
        encoder_kernel_grad_kernel(enc_back, enc_reach, enc_reach, counts, *refs)

    gexpand_e = slot(gexpand_e, dec_reduce)
    keep_e, send_e = call(
        kernel_grad_body,
        micro,
        [gmixed_e, low, high, enc_back_masks, second_e],
        [gexpand_e],
        [],
        packed_pair((ENC_TAPS + 2) * shard_part),
        extended_scratch + [((inner_width, ENC_TAPS * inner_width), F32)],
        ENC_TAPS * tap_unit,
        place=place,
    )

    def encoder_back_body(*refs):
        encoder_back_kernel(enc_back, enc_reach, enc_reach, counts, *refs)

    enc_reduce = Chain(reduce_pieces(keep_e, send_e))
    def encoder_back_body(*refs):
        encoder_back_kernel(enc_back, enc_reach, enc_reach, *refs)

    chains = [dec_reduce, enc_reduce]
    early = (micro + 1) // 2
    spans = [(0, early)] + ([(early, micro - early)] if micro > early else [])
    ghidden, conv_sums = (), []
    for offset, count in spans:
        enc_inner, ghidden, conv_sums = slot((enc_inner, ghidden, conv_sums), *chains)
        *ghidden, conv_part = call(
            encoder_back_body,
            count,
            [gmixed_e, low, high, enc_back_masks, hidden_e],
            [enc_flat, enc_inner],
            [(inner_shape, BF16)],
            [((3, 8, inner_width), F32)],
            extended_scratch + [((rows, inner_width), F32)],
            ENC_TAPS * tap_unit * count // micro,
            offset=offset,
            carried=ghidden,
        )
        conv_sums.append(conv_part)
    (ghidden_e,), conv_inner_e = ghidden, sum(conv_sums)

    def project_grad_body(*refs):
        project_grad_kernel(counts, *refs)

    keep_p, send_p = call(
        project_grad_body,
        micro,
        [first_e, ghidden_e],
        [],
        [],
        packed_pair(width // fsdp_count),
        [((width, inner_width), F32)],
        unit,
        place=place,
    )
    entry_reduce = Chain(reduce_pieces(keep_p, send_p))
    chains.append(entry_reduce)
    gstream, leave_sums = (), []
    for offset, count in spans:
        enc_wide, gstream, leave_sums = slot((enc_wide, gstream, leave_sums), *chains)
        *gstream, leave_wide = call(
            leave_kernel,
            count,
            [ghidden_e, stream, gmiddle],
            [enc_project, enc_wide],
            [(wide_shape, BF16)],
            [((2, 8, width), F32)],
            [((rows, width), F32)],
            unit * count // micro,
            offset=offset,
            carried=gstream,
        )
        leave_sums.append(leave_wide)

    def row_sums(entry):
        sums = jnp.sum(entry, axis=1)
        return jnp.pad(sums, ((0, 0), (0, width - sums.shape[1])))

    sums = [sum(leave_sums), link_wide, turn_wide]
    sums += [conv_inner_e, link_inner, conv_inner_d, turn_inner]
    vector_reduce = Chain(reduce_vectors(jnp.concatenate([row_sums(entry) for entry in sums])))
    chains.append(vector_reduce)
    output = ()
    for offset, count in spans:
        dec_wide, gstream, output = slot((dec_wide, gstream, output), *chains)
        output = call(
            output_kernel,
            count,
            [third_d, middle],
            [dec_expand, dec_wide],
            [(wide_shape, BF16)],
            [],
            [((rows, width), F32)],
            unit * count // micro,
            offset=offset,
            carried=output,
        )
    def own_columns(vectors):
        part = vectors.shape[1] // fsdp_count
        return lax.dynamic_slice_in_dim(vectors, own * part, part, axis=1)

    project_rows = width // fsdp_count
    scale = total_rows**-0.5
    shapes = {
        "project": (project_rows, inner_width),
        "expand": (shard_part, width),
    }

    def finish(chain, names):
        pieces, indices = chain.finish()
        layout, outs, start = [], [], 0
        for name in names:
            shape = shapes.get(name, (name, shard_part, inner_width))
            layout.append((start, name == "expand"))
            outs.append(jax.ShapeDtypeStruct(shape, F32))
            size = 1
            for extent in shape:
                size *= extent
            start += size // inner_width

        def body(*refs):
            finish_kernel(layout, scale, indices, *refs)

        whole = pl.BlockSpec(memory_space=pltpu.VMEM)
        return pl.pallas_call(
            body,
            in_specs=[pl.BlockSpec(memory_space=pltpu.SMEM)] + [whole] * len(pieces),
            out_specs=[whole] * len(outs),
            out_shape=outs,
            scratch_shapes=[pltpu.VMEM((seq_count,) + pieces[0].shape[1:], BF16)],
            compiler_params=pltpu.CompilerParams(vmem_limit_bytes=VMEM_LIMIT),
        )(place, *pieces)

    names = [["project", DEC_TAPS, "expand"], [ENC_TAPS, "expand"], ["project"]]
    finished = [None] * len(names)
    while any(chain.pending is not None for chain in chains):
        for index, entry in enumerate(names):
            if finished[index] is None and chains[index].pending is None:
                finished[index] = finish(chains[index], entry)
        output, finished = slot((output, finished), *chains)
    finished = [entry or finish(chain, kinds) for entry, chain, kinds in zip(finished, chains, names)]
    sums = vector_reduce.finish() * factor
    wide_sums = sums[:6]
    order = [wide_sums[:2], wide_sums[4:5], wide_sums[2:4], wide_sums[5:]]
    wide_own = own_columns(jnp.concatenate(order))
    inner_own = own_columns(sums[6:, :inner_width])

    def vectors(wide_rows, inner_rows):
        widegain = wide_rows[0]
        wideshift = wide_rows[1:3]
        gains = jnp.stack([inner_rows[0], inner_rows[3]])
        shifts = jnp.stack([inner_rows[1], inner_rows[4], inner_rows[2], inner_rows[5]])
        return widegain, gains, wideshift, shifts

    (gproject_d, gkernel_d, gexpand_d), (gkernel_e, gexpand_e), (gproject_e,) = finished
    return (
        output[0][:, None],
        gstream[0][:, None],
        gproject_e,
        gkernel_e,
        gexpand_e,
        *vectors(wide_own[:3], inner_own[:6]),
        gproject_d,
        gkernel_d,
        gexpand_d,
        *vectors(wide_own[3:], inner_own[6:]),
    )


def solution(mesh):
    tokens = P(None, "fsdp", "seq", None)
    weights = (
        P("fsdp", None),
        P(None, "fsdp", None),
        P("fsdp", None),
        P("fsdp"),
        P(None, "fsdp"),
        P(None, "fsdp"),
        P(None, "fsdp"),
    )
    return jax.shard_map(
        local,
        mesh=mesh,
        in_specs=(tokens, P(None, "fsdp", None), tokens) + weights + weights,
        out_specs=(tokens, tokens) + weights + weights,
        check_vma=False,
    )
```

```python
import jax
import jax.numpy as jnp
from jax import lax
from jax.experimental import pallas as pl
from jax.experimental.pallas import tpu as pltpu
from jax.sharding import PartitionSpec as P

ENC_TAPS = 5
ENC_DILATION = 8
DEC_TAPS = 3
DEC_DILATION = 16
EPSILON = 1e-05
CHUNK = 48
VMEM_LIMIT = 60 * 1024 * 1024

BF16 = jnp.bfloat16
F32 = jnp.float32
NN = (((1,), (0,)), ((), ()))
NT = (((1,), (1,)), ((), ()))
TN = (((0,), (0,)), ((), ()))


def dot(left, right, dims):
    return lax.dot_general(left, right, dims, preferred_element_type=F32)


def tap_offsets(encoder):
    if encoder:
        return [(tap - ENC_TAPS // 2) * ENC_DILATION for tap in range(ENC_TAPS)]
    return [(tap - DEC_TAPS + 1) * DEC_DILATION for tap in range(DEC_TAPS)]


def normalized(values):
    average = jnp.mean(values, axis=-1, keepdims=True)
    centred = values - average
    scale = lax.rsqrt(jnp.mean(centred * centred, axis=-1, keepdims=True) + EPSILON)
    return centred * scale, scale


def norm_silu(values, gain, shift):
    unit, _ = normalized(values)
    half = unit * gain + shift
    return half * (1.0 + jnp.tanh(half))


def norm_silu_back(values, gain, shift, grad):
    unit, scale = normalized(values)
    half = unit * gain + shift
    slope = jnp.tanh(half)
    grad_inner = grad * ((1.0 + slope) * (1.0 + half * (1.0 - slope)))
    grad_unit = grad_inner * gain
    along = jnp.mean(grad_unit * unit, axis=-1, keepdims=True)
    level = jnp.mean(grad_unit, axis=-1, keepdims=True)
    grad_values = scale * (grad_unit - level - unit * along)
    return grad_values, grad_inner * unit, grad_inner


def fold_rows(values):
    total = values[0:8]
    for start in range(8, values.shape[0], 8):
        total = total + values[start : start + 8]
    return total


def by_chunks(row_count, body):
    for start in range(0, row_count, CHUNK):
        body(pl.ds(start, CHUNK))


def clear_first(*refs):
    @pl.when(pl.program_id(0) == 0)
    def _():
        for ref in refs:
            ref[...] = jnp.zeros_like(ref)


def at_last(body):
    pl.when(pl.program_id(0) == pl.num_programs(0) - 1)(body)


def fill_columns(columns, extended, masks, offsets, front, row_count):
    width = extended.shape[-1]
    for tap, offset in enumerate(offsets):
        window = extended[front + offset : front + offset + row_count, :]
        if offset != 0:
            window = window * masks[:, tap : tap + 1]
        columns[:, tap * width : (tap + 1) * width] = window


def enter_kernel(stream, project, wide, inner, first, hidden, second):
    row_count = stream.shape[0]

    def make_first(rows):
        values = stream[rows, :].astype(F32)
        first[rows, :] = norm_silu(values, wide[0:1, :], wide[1:2, :]).astype(BF16)

    by_chunks(row_count, make_first)
    hidden[...] = dot(first[...], project[...], NN) + inner[4:5, :]

    def make_second(rows):
        second[rows, :] = norm_silu(hidden[rows, :], inner[0:1, :], inner[2:3, :]).astype(BF16)

    by_chunks(row_count, make_second)


def fetch(sources, spots, target, semaphores):
    copies = [
        pltpu.make_async_copy(source, target.at[spot], semaphores.at[index])
        for index, (source, spot) in enumerate(zip(sources, spots))
    ]
    for copy in copies:
        copy.start()
    for copy in copies:
        copy.wait()


def fetch_shards(place, own, parts, pieces, origins, landed, semaphores):
    sources, spots = [], []
    for piece, entries in zip(pieces, origins):
        for index, (far, differs) in enumerate(entries):
            sources.append(piece.at[index])
            spots.append((place[0] ^ far) * parts + (own ^ differs))
    fetch(sources, spots, landed, semaphores)


class Shards:
    def __init__(self, landed, fsdp_count):
        self.landed, self.fsdp_count = landed, fsdp_count
        self.seq_count = landed.shape[0] // fsdp_count

    def spread(self, shard, start, rows, write):
        part, done = self.landed.shape[1], 0
        while done < rows:
            owner, local = (start + done) // part, (start + done) % part
            size = min(rows - done, part - local)
            write(done, self.landed[shard * self.seq_count + owner, local : local + size, :])
            done += size


def enter_encoder_kernel(origins, spacing, place, stream, *refs):
    pieces, refs = refs[:-8], refs[-8:]
    wide, inner, first, hidden, second, project, landed, semaphores = refs

    @pl.when(pl.program_id(0) == 0)
    def _():
        fetch_shards(place, place[1], PARTS, pieces, origins, landed, semaphores)
        shard_rows = project.shape[0] * PARTS // landed.shape[0]
        part = shard_rows - (PARTS - 1) * spacing
        for index in range(landed.shape[0]):
            start = index // PARTS * shard_rows + index % PARTS * spacing
            project[start : start + part, :] = landed[index, :part, :]

    enter_kernel(stream, project, wide, inner, first, hidden, second)


def unpack_kernel(shards, start, taps, kernel, flat):
    width = flat.shape[0]
    part = width // shards.fsdp_count
    for own in range(shards.fsdp_count):
        for tap in range(taps):

            def write(done, block):
                row = own * part + done
                size = block.shape[0]
                kernel[tap * width + row : tap * width + row + size, :] = block
                flat[row : row + size, tap * width : (tap + 1) * width] = block

            shards.spread(own, start + tap * part, part, write)


def unpack_expand(shards, start, expand):
    width = expand.shape[1] // 2
    part = expand.shape[0] // shards.fsdp_count
    for own in range(shards.fsdp_count):
        for half in range(2):

            def write(done, block):
                row = own * part + done
                expand[row : row + block.shape[0], half * width : (half + 1) * width] = block

            shards.spread(own, start + half * part, part, write)


def unpack_rows(shards, start, whole):
    part = whole.shape[0] // shards.fsdp_count
    for own in range(shards.fsdp_count):

        def write(done, block):
            row = own * part + done
            whole[row : row + block.shape[0], :] = block

        shards.spread(own, start, part, write)


def middle_kernel(offsets, counts, origins, place, second_in, low, high, masks, stream, *refs):
    pieces, refs = refs[:-13], refs[-13:]
    enc_wide, enc_inner, mixed, third, middle, expand, flat, project = refs[:8]
    extended, columns, kernel, landed, semaphores = refs[8:]
    row_count = stream.shape[0]
    front = low.shape[0]

    @pl.when(pl.program_id(0) == 0)
    def _():
        seq_count, fsdp_count = counts
        fetch_shards(place, place[2], seq_count, pieces, origins, landed, semaphores)
        shards = Shards(landed, fsdp_count)
        unpack_kernel(shards, 0, len(offsets), kernel, flat)
        start = kernel.shape[0] // fsdp_count
        unpack_expand(shards, start, expand)
        unpack_rows(shards, start + expand.shape[0] * 2 // fsdp_count, project)

    extended[:front, :] = low[...]
    extended[front : front + row_count, :] = second_in[...]
    extended[front + row_count :, :] = high[...]
    fill_columns(columns, extended, masks, offsets, front, row_count)
    mixed[...] = dot(columns[...], kernel[...], NN) + enc_inner[5:6, :]

    def make_third(rows):
        third[rows, :] = norm_silu(mixed[rows, :], enc_inner[1:2, :], enc_inner[3:4, :]).astype(
            BF16
        )

    by_chunks(row_count, make_third)
    middle[...] = dot(third[...], expand[...], NN)

    def make_middle(rows):
        branch = middle[rows, :] + enc_wide[2:3, :]
        middle[rows, :] = stream[rows, :].astype(F32) + branch

    by_chunks(row_count, make_middle)


def turn_kernel(offsets, counts, origins, place, second, low, masks, cotangent, *refs):
    pieces, refs = refs[:-16], refs[-16:]
    inner, third, grad_mixed, grad_expand, flat, expand, sums_wide, sums_inner = refs[:8]
    extended, columns, mixed, grad_third, total, kernel, landed, semaphores = refs[8:]
    row_count = cotangent.shape[0]
    front = low.shape[0]
    clear_first(total, sums_wide, sums_inner)

    @pl.when(pl.program_id(0) == 0)
    def _():
        seq_count, fsdp_count = counts
        fetch_shards(place, place[2], seq_count, pieces, origins, landed, semaphores)
        shards = Shards(landed, fsdp_count)
        unpack_kernel(shards, 0, len(offsets), kernel, flat)
        unpack_expand(shards, kernel.shape[0] // fsdp_count, expand)

    extended[:front, :] = low[...]
    extended[front : front + row_count, :] = second[...]
    fill_columns(columns, extended, masks, offsets, front, row_count)
    mixed[...] = dot(columns[...], kernel[...], NN) + inner[5:6, :]

    def make_third(rows):
        third[rows, :] = norm_silu(mixed[rows, :], inner[1:2, :], inner[3:4, :]).astype(BF16)

    by_chunks(row_count, make_third)
    grad_third[...] = dot(cotangent[...], expand[...], NT)

    def add_cotangent(rows):
        sums_wide[0] += fold_rows(cotangent[rows, :].astype(F32))

    by_chunks(row_count, add_cotangent)

    def make_grad(rows):
        grad, gain_part, shift_part = norm_silu_back(
            mixed[rows, :], inner[1:2, :], inner[3:4, :], grad_third[rows, :]
        )
        rounded = grad.astype(BF16)
        grad_mixed[rows, :] = rounded
        sums_inner[0] += fold_rows(gain_part)
        sums_inner[1] += fold_rows(shift_part)
        sums_inner[2] += fold_rows(rounded.astype(F32))

    by_chunks(row_count, make_grad)
    total[...] += dot(third[...], cotangent[...], TN)

    @at_last
    def _():
        grad_expand[...] = total[...].astype(BF16)


def routes(seq_count):
    rest = [1 << bit for bit in range(1, seq_count.bit_length() - 1)]
    return rest[::-1], rest


def pack(place, sections, keep, send):
    seq_count, fsdp_count, part = sections.seq_count, sections.fsdp_count, keep.shape[1]
    orders = routes(seq_count)
    cells = keep.shape[0] // 2

    def write(own_core):
        for shard in range(fsdp_count):
            far = place[0] ^ shard
            half = far // (fsdp_count // 2)
            within = far % (fsdp_count // 2)
            for owner in range(seq_count):
                differs = place[2] ^ owner
                spots = []
                for order in orders:
                    spot = 0
                    for bit in order:
                        spot = spot * 2 + (differs // bit) % 2
                    spots.append(spot)
                spot = jnp.where(half == 0, spots[0], spots[1])
                spot = half * cells + spot * (fsdp_count // 2) + within
                target = keep if owner % 2 == own_core else send
                filled = 0
                for start, rows, block in sections.cut(owner * part, part):
                    target[spot, filled : filled + rows, :] = block(shard, start, rows)
                    filled += rows
                if filled < part:
                    target[spot, filled:, :] = jnp.zeros((part - filled, keep.shape[2]), BF16)

    for own_core in range(2):

        @pl.when(place[2] % 2 == own_core)
        def _():
            write(own_core)


class Sections:
    def __init__(self, seq_count, fsdp_count):
        self.seq_count, self.fsdp_count = seq_count, fsdp_count
        self.entries = []

    def add(self, rows, block):
        self.entries.append((rows, block))

    def rows_of(self, total):
        part = total.shape[0] // self.fsdp_count
        self.add(
            part,
            lambda shard, start, rows: total[
                shard * part + start : shard * part + start + rows, :
            ].astype(BF16),
        )

    def kernel(self, total, taps):
        part, width = total.shape[0] // self.fsdp_count, total.shape[1] // taps
        for tap in range(taps):
            self.add(
                part,
                lambda shard, start, rows, tap=tap: total[
                    shard * part + start : shard * part + start + rows,
                    tap * width : (tap + 1) * width,
                ].astype(BF16),
            )

    def cut(self, first, rows):
        found, begin = [], 0
        for length, block in self.entries:
            low, high = max(first, begin), min(first + rows, begin + length)
            if low < high:
                found.append((low - begin, high - low, block))
            begin += length
        return found


def back_columns(offsets, front, back, grad_mixed, low, high, masks, extended, columns):
    row_count = grad_mixed.shape[0]
    if front:
        extended[:front, :] = low[...]
    extended[front : front + row_count, :] = grad_mixed[...]
    if back:
        extended[front + row_count :, :] = high[...]
    fill_columns(columns, extended, masks, offsets, front, row_count)


def hidden_grad(hidden, inner, grad_second, grad_hidden, sums_inner):
    def make_grad(rows):
        grad, gain_part, shift_part = norm_silu_back(
            hidden[rows, :], inner[0:1, :], inner[2:3, :], grad_second[rows, :]
        )
        rounded = grad.astype(BF16)
        grad_hidden[rows, :] = rounded
        sums_inner[0] += fold_rows(gain_part)
        sums_inner[1] += fold_rows(shift_part)
        sums_inner[2] += fold_rows(rounded.astype(F32))

    by_chunks(hidden.shape[0], make_grad)


def decoder_back_kernel(
    offsets,
    back,
    counts,
    place,
    grad_mixed,
    high,
    masks,
    second,
    hidden,
    first,
    flat,
    inner,
    grad_expand,
    grad_hidden,
    keep,
    send,
    sums_inner,
    extended,
    columns,
    grad_second,
    total_kernel,
    total_project,
):
    clear_first(total_kernel, total_project, sums_inner)
    back_columns(offsets, 0, back, grad_mixed, None, high, masks, extended, columns)
    grad_second[...] = dot(columns[...], flat[...], NT)
    hidden_grad(hidden, inner, grad_second, grad_hidden, sums_inner)
    total_kernel[...] += dot(second[...], columns[...], TN)
    total_project[...] += dot(first[...], grad_hidden[...], TN)

    @at_last
    def _():
        sections = Sections(*counts)
        sections.rows_of(total_project)
        sections.kernel(total_kernel, len(offsets))
        sections.kernel(grad_expand, 2)
        pack(place, sections, keep, send)


def encoder_kernel_grad_kernel(
    offsets,
    front,
    back,
    counts,
    place,
    grad_mixed,
    low,
    high,
    masks,
    second,
    grad_expand,
    keep,
    send,
    extended,
    columns,
    total_kernel,
):
    clear_first(total_kernel)
    back_columns(offsets, front, back, grad_mixed, low, high, masks, extended, columns)
    total_kernel[...] += dot(second[...], columns[...], TN)

    @at_last
    def _():
        sections = Sections(*counts)
        sections.kernel(total_kernel, len(offsets))
        sections.kernel(grad_expand, 2)
        pack(place, sections, keep, send)


def encoder_back_kernel(
    offsets,
    front,
    back,
    grad_mixed,
    low,
    high,
    masks,
    hidden,
    flat,
    inner,
    grad_hidden,
    sums_inner,
    extended,
    columns,
    grad_second,
):
    clear_first(sums_inner)
    back_columns(offsets, front, back, grad_mixed, low, high, masks, extended, columns)
    grad_second[...] = dot(columns[...], flat[...], NT)
    hidden_grad(hidden, inner, grad_second, grad_hidden, sums_inner)


def project_grad_kernel(counts, place, first, grad_hidden, keep, send, total):
    clear_first(total)
    total[...] += dot(first[...], grad_hidden[...], TN)

    @at_last
    def _():
        sections = Sections(*counts)
        sections.rows_of(total)
        pack(place, sections, keep, send)


def link_back_kernel(
    grad_hidden,
    middle,
    cotangent,
    mixed,
    third,
    project,
    dec_wide,
    expand,
    enc_inner,
    grad_middle,
    grad_mixed,
    grad_expand,
    sums_wide,
    sums_inner,
    grad_first,
    branch,
    grad_third,
    total,
):
    row_count = middle.shape[0]
    clear_first(total, sums_wide, sums_inner)
    grad_first[...] = dot(grad_hidden[...], project[...], NT)

    def make_branch(rows):
        grad, gain_part, shift_part = norm_silu_back(
            middle[rows, :], dec_wide[0:1, :], dec_wide[1:2, :], grad_first[rows, :]
        )
        sums_wide[0] += fold_rows(gain_part)
        sums_wide[1] += fold_rows(shift_part)
        grad = cotangent[rows, :].astype(F32) + grad
        grad_middle[rows, :] = grad
        rounded = grad.astype(BF16)
        branch[rows, :] = rounded
        sums_wide[2] += fold_rows(rounded.astype(F32))

    by_chunks(row_count, make_branch)
    grad_third[...] = dot(branch[...], expand[...], NT)

    def make_grad(rows):
        grad, gain_part, shift_part = norm_silu_back(
            mixed[rows, :], enc_inner[1:2, :], enc_inner[3:4, :], grad_third[rows, :]
        )
        rounded = grad.astype(BF16)
        grad_mixed[rows, :] = rounded
        sums_inner[0] += fold_rows(gain_part)
        sums_inner[1] += fold_rows(shift_part)
        sums_inner[2] += fold_rows(rounded.astype(F32))

    by_chunks(row_count, make_grad)
    total[...] += dot(third[...], branch[...], TN)

    @at_last
    def _():
        grad_expand[...] = total[...].astype(BF16)


def output_kernel(third, middle, expand, wide, output, branch):
    branch[...] = dot(third[...], expand[...], NN)

    def make_output(rows):
        values = middle[rows, :] + (branch[rows, :] + wide[2:3, :])
        output[rows, :] = values.astype(BF16)

    by_chunks(middle.shape[0], make_output)


def leave_kernel(
    grad_hidden, stream, grad_middle, project, wide, grad_stream, sums_wide, grad_first
):
    row_count = stream.shape[0]
    clear_first(sums_wide)
    grad_first[...] = dot(grad_hidden[...], project[...], NT)

    def make_grad(rows):
        grad, gain_part, shift_part = norm_silu_back(
            stream[rows, :].astype(F32), wide[0:1, :], wide[1:2, :], grad_first[rows, :]
        )
        sums_wide[0] += fold_rows(gain_part)
        sums_wide[1] += fold_rows(shift_part)
        grad_stream[rows, :] = (grad_middle[rows, :] + grad).astype(BF16)

    by_chunks(row_count, make_grad)


def finish_kernel(layout, factor, indices, place, *refs):
    count = len(indices)
    pieces, outs, landed = refs[:count], refs[count:-1], refs[-1]
    part = landed.shape[1]
    for piece, entries in zip(pieces, indices):
        for spot, index in enumerate(entries):
            landed[place[2] ^ index] = piece[spot]

    def write(out, where, columns, start, rows):
        done = 0
        while done < rows:
            owner, local = (start + done) // part, (start + done) % part
            size = min(rows - done, part - local)
            block = landed[owner, local : local + size, :].astype(F32) * factor
            if where is None:
                out[done : done + size, columns] = block
            else:
                out[where, done : done + size, :] = block
            done += size

    for out, (start, halves) in zip(outs, layout):
        width = landed.shape[2]
        if halves:
            for half in range(2):
                columns = slice(half * width, (half + 1) * width)
                write(out, None, columns, start + half * out.shape[0], out.shape[0])
        elif len(out.shape) == 3:
            for tap in range(out.shape[0]):
                write(out, tap, None, start + tap * out.shape[1], out.shape[1])
        else:
            write(out, None, slice(0, width), start, out.shape[0])


def stepped(array, offset):
    rest = (0,) * (array.ndim - 1)
    return pl.BlockSpec((None,) + array.shape[1:], lambda step: (step + offset,) + rest)


def held(array):
    zeros = (0,) * array.ndim
    return pl.BlockSpec(array.shape, lambda step: zeros, pipeline_mode=pl.Buffered(1))


def call(
    body,
    steps,
    moving,
    fixed,
    outs,
    sums,
    scratch,
    flops,
    loose=(),
    place=None,
    semaphores=0,
    offset=0,
    carried=(),
):
    out_shapes = [jax.ShapeDtypeStruct(shape, kind) for shape, kind in outs]
    sum_shapes = [jax.ShapeDtypeStruct(shape, kind) for shape, kind in sums]
    operands = list(moving) + list(loose) + list(fixed)
    traffic = sum(
        entry.size * entry.dtype.itemsize for entry in operands + out_shapes + sum_shapes
    )
    in_specs = [stepped(entry, offset) for entry in moving]
    in_specs += [pl.BlockSpec(memory_space=pl.ANY) for _ in loose]
    in_specs += [held(entry) for entry in fixed]
    if place is not None:
        operands = [place] + operands
        in_specs = [pl.BlockSpec(memory_space=pltpu.SMEM)] + in_specs
    count = len(operands)
    operands += list(carried)
    in_specs += [pl.BlockSpec(memory_space=pl.ANY) for _ in carried]
    scratch_shapes = [pltpu.VMEM(shape, kind) for shape, kind in scratch]
    if semaphores:
        scratch_shapes.append(pltpu.SemaphoreType.DMA((semaphores,)))

    def kernel(*refs):
        body(*refs[:count], *refs[count + len(carried) :])

    return pl.pallas_call(
        kernel,
        grid=(steps,),
        in_specs=in_specs,
        out_specs=[stepped(entry, offset) for entry in out_shapes]
        + [held(entry) for entry in sum_shapes],
        out_shape=out_shapes + sum_shapes,
        scratch_shapes=scratch_shapes,
        input_output_aliases={count + index: index for index in range(len(carried))},
        compiler_params=pltpu.CompilerParams(
            dimension_semantics=("arbitrary",), vmem_limit_bytes=VMEM_LIMIT
        ),
        cost_estimate=pl.CostEstimate(flops=flops, bytes_accessed=traffic, transcendentals=0),
    )(*operands)


def owners(places, doc_ends):
    return jnp.sum((places[..., None] >= doc_ends[:, None, :]).astype(jnp.int32), axis=-1)


def build_masks(places, doc_ends, stream_len, offsets):
    own_doc = owners(places[None, :], doc_ends)
    columns = []
    for offset in offsets:
        partner = places + offset
        inside = (partner >= 0) & (partner < stream_len)
        columns.append(inside[None, :] & (owners(partner[None, :], doc_ends) == own_doc))
    return jnp.stack(columns, axis=-1).astype(BF16)


def to_next(block):
    count = lax.axis_size("seq")
    return lax.ppermute(block, "seq", [(i, i + 1) for i in range(count - 1)])


def to_previous(block):
    count = lax.axis_size("seq")
    return lax.ppermute(block, "seq", [(i + 1, i) for i in range(count - 1)])


def exchanged(block, axis, bit):
    return lax.ppermute(block, axis, [(i, i ^ bit) for i in range(lax.axis_size(axis))])


def round_up(value, unit):
    return -(-value // unit) * unit


def padded(block, rows):
    return jnp.pad(block, ((0, rows - block.shape[0]), (0, 0)))


class Chain:
    def __init__(self, steps):
        self.steps, self.result = steps, None
        self.pending = next(steps)

    def advance(self, arrays=None):
        try:
            self.pending = self.steps.send(self.pending if arrays is None else arrays)
        except StopIteration as stop:
            self.pending, self.result = None, stop.value
        return self

    def finish(self):
        while self.pending is not None:
            self.advance()
        return self.result


def slot(operand, *chains):
    live = [chain for chain in chains if chain.pending is not None]
    operand, arrays = lax.optimization_barrier((operand, [chain.pending for chain in live]))
    for chain, pending in zip(live, arrays):
        chain.advance(pending)
    return operand


PARTS = 4


def half_spacing(rows):
    part = round_up(rows // PARTS, 16)
    return part, (rows - part) // (PARTS - 1)


def tiled(block):
    return block.reshape(block.shape[0] // 8, 8, block.shape[1])


class Spread:
    def __init__(self, columns, fars, bits):
        self.parts = [jnp.stack(columns)]
        self.bits, self.step = bits, 0
        self.origins = [(far, 0) for far in fars]
        self.arrays, self.all_origins = [], []

    def moved(self, entries, bit):
        return [(far, differs ^ bit) for far, differs in entries]

    def advance(self, block):
        bit = self.bits[self.step]
        other = exchanged(block, "seq", bit)
        more = self.moved(self.origins, bit)
        self.step += 1
        if self.step < len(self.bits):
            self.parts = [block, other]
            self.origins = self.origins + more
        else:
            self.arrays = [other, block, exchanged(block, "seq", 1)]
            self.all_origins = [more, self.origins, self.moved(self.origins, 1)]

    def cross(self, arrays):
        self.arrays = arrays + [exchanged(arrays[0], "seq", 1)]
        self.all_origins.append(self.moved(self.all_origins[0], 1))


def move(spreads, crossing, before=(), after=()):
    parts, arrays, after = lax.optimization_barrier(
        ([entry.parts for entry in spreads], [entry.arrays for entry in crossing], after)
    )
    blocks = [jnp.concatenate(pair, axis=0) if len(pair) > 1 else pair[0] for pair in parts]
    blocks, arrays, before = lax.optimization_barrier((blocks, arrays, before))
    for entry, block in zip(spreads, blocks):
        entry.advance(block)
    for entry, own in zip(crossing, arrays):
        entry.cross(own)
    return tuple(before) + tuple(after)


def in_progress(spreads):
    return spreads[0].step < len(spreads[0].bits) - 1


def received(spreads):
    arrays = [
        array.reshape(array.shape[0], -1, array.shape[-1])
        for entry in spreads
        for array in entry.arrays
    ]
    origins = [entries for entry in spreads for entries in entry.all_origins]
    return arrays, origins


def along_fsdp(block, fars=None):
    fars = range(1, lax.axis_size("fsdp")) if fars is None else fars
    return [block] + [exchanged(block, "fsdp", far) for far in fars]


def spread_pair(columns):
    orders = routes(lax.axis_size("seq"))
    middle = len(columns) // 2
    return [
        Spread(columns[:middle], range(middle), orders[0]),
        Spread(columns[middle:], range(middle, len(columns)), orders[1]),
    ]


def half_piece(shard):
    part, spacing = half_spacing(shard.shape[0])
    own = lax.axis_index("seq") & (PARTS - 1)
    return lax.dynamic_slice_in_dim(shard, own * spacing, part, axis=0)


def full_piece(shard):
    seq_count = lax.axis_size("seq")
    part = round_up(shard.shape[0], 8 * seq_count) // seq_count
    return tiled(
        lax.dynamic_slice_in_dim(
            padded(shard, part * seq_count), lax.axis_index("seq") * part, part, axis=0
        )
    )


def add_low(*blocks):
    total = blocks[0].astype(F32)
    for block in blocks[1:]:
        total = total + block.astype(F32)
    return total.astype(BF16)


def reduce_pieces(keep, send):
    seq_count, fsdp_count = lax.axis_size("seq"), lax.axis_size("fsdp")
    shape = (2, -1, fsdp_count // 2) + keep.shape[1:]
    (send,) = yield [send]
    parts = (keep.reshape(shape), exchanged(send, "seq", 1).reshape(shape))
    orders = routes(seq_count)
    terms = [[entry[half] for entry in parts] for half in range(2)]
    for step in range(len(orders[0])):
        size = terms[0][0].shape[0] // 2
        leaving = [add_low(*[term[size:] for term in entries]) for entries in terms]
        leaving = yield leaving
        terms = [
            [term[:size] for term in entries] + [exchanged(block, "seq", order[step])]
            for entries, block, order in zip(terms, leaving, orders)
        ]
    columns = []
    for entries in terms:
        columns += [[term[0, within] for term in entries] for within in range(fsdp_count // 2)]
    leaving = yield [add_low(*columns[far]) for far in range(1, fsdp_count)]
    arrived = [exchanged(block, "fsdp", far + 1) for far, block in enumerate(leaving)]
    block, indices = add_low(*columns[0], *arrived)[None], [0]
    for bit in orders[1]:
        (block,) = yield [block]
        block = jnp.concatenate([block, exchanged(block, "seq", bit)], axis=0)
        indices = indices + [index ^ bit for index in indices]
    (block,) = yield [block]
    return [block, exchanged(block, "seq", 1)], [indices, [index ^ 1 for index in indices]]


def reduce_vectors(vectors):
    for axis in ("seq", "fsdp"):
        bit = 1
        while bit < lax.axis_size(axis):
            (vectors,) = yield [vectors]
            vectors = vectors + exchanged(vectors, axis, bit)
            bit *= 2
    return vectors


def local(
    characters,
    lengths,
    cotangent,
    encproject,
    enckernel,
    encexpand,
    encwidegain,
    encgains,
    encwideshift,
    encshifts,
    decproject,
    deckernel,
    decexpand,
    decwidegain,
    decgains,
    decwideshift,
    decshifts,
):
    micro, _, rows, width = characters.shape
    inner_width = encproject.shape[1]
    seq_count = lax.axis_size("seq")
    fsdp_count = lax.axis_size("fsdp")
    stream_len = rows * seq_count
    total_rows = micro * stream_len * fsdp_count
    factor = 1.0 / jnp.sqrt(jnp.float32(total_rows))
    stream = characters[:, 0]
    cot = cotangent[:, 0]

    seq_index = lax.axis_index("seq")
    place = jnp.stack([lax.axis_index("fsdp"), seq_index & (PARTS - 1), seq_index])
    place = place.astype(jnp.int32)
    def rows_of(kernel):
        return kernel.reshape(-1, kernel.shape[2])

    def halves(expand):
        return [expand[:, :inner_width], expand[:, inner_width:]]

    wide_local = [encwidegain[None], encwideshift, decwidegain[None], decwideshift]
    wide_local = jnp.concatenate(wide_local, axis=0)
    inner_local = jnp.concatenate([encgains, encshifts, decgains, decshifts], axis=0)
    vector_local = jnp.concatenate([wide_local.reshape(-1), inner_local.reshape(-1)])
    enc_rows = jnp.concatenate([rows_of(enckernel)] + halves(encexpand) + [decproject], axis=0)
    dec_rows = jnp.concatenate([rows_of(deckernel)] + halves(decexpand), axis=0)
    _, spacing = half_spacing(encproject.shape[0])
    counts = (seq_count, fsdp_count)
    enc_own, dec_own = full_piece(enc_rows), full_piece(dec_rows)
    vector_rows = round_up(vector_local.size, 8 * inner_width) // inner_width
    vector_piece = jnp.pad(vector_local, (0, vector_rows * inner_width - vector_local.size))
    vector_piece = vector_piece.reshape(vector_rows, inner_width)
    entry_piece = jnp.concatenate([half_piece(encproject), vector_piece], axis=0)
    entry_columns = along_fsdp(tiled(entry_piece))
    entry_spread = Spread(entry_columns, range(fsdp_count), [2])
    move([entry_spread], [])
    enc_spreads = spread_pair(along_fsdp(enc_own))
    vector_shards = jnp.stack(
        [column[-vector_rows // 8 :].reshape(-1)[: vector_local.size] for column in entry_columns]
    )
    own = lax.axis_index("fsdp")
    vector_shards = jnp.stack(
        [
            lax.dynamic_index_in_dim(vector_shards, own ^ shard, 0, keepdims=False)
            for shard in range(fsdp_count)
        ]
    ).astype(F32)

    def whole_vectors(shards, like):
        cut = shards.reshape((fsdp_count,) + like.shape)
        return jnp.transpose(cut, (1, 0, 2)).reshape(like.shape[0], -1)

    wides = whole_vectors(vector_shards[:, : wide_local.size], wide_local)
    inners = whole_vectors(vector_shards[:, wide_local.size :], inner_local)
    wides = wides * jnp.array([0.5, 0.5, 1.0] * 2, F32)[:, None]
    inners = inners * jnp.array(([0.5] * 4 + [1.0] * 2) * 2, F32)[:, None]
    enc_wide, dec_wide = wides[:3], wides[3:]
    enc_inner, dec_inner = inners[:6], inners[6:]

    far_half = fsdp_count // 2 + 1
    (dec_own,) = move(enc_spreads, [entry_spread], (dec_own,))
    dec_columns = along_fsdp(dec_own, range(1, far_half))
    project_pieces, entry_origins = received([entry_spread])
    while in_progress(enc_spreads):
        move(enc_spreads, [])

    def landing(pieces):
        count = sum(piece.shape[0] for piece in pieces)
        return ((count,) + pieces[0].shape[1:], BF16), count

    places = lax.axis_index("seq") * rows + jnp.arange(rows, dtype=jnp.int32)
    doc_ends = jnp.cumsum(lengths[:, 0], axis=1)
    enc_offsets = tap_offsets(True)
    dec_offsets = tap_offsets(False)
    enc_back = [-offset for offset in enc_offsets]
    dec_back = [-offset for offset in dec_offsets]
    enc_masks = build_masks(places, doc_ends, stream_len, enc_offsets)
    dec_masks = build_masks(places, doc_ends, stream_len, dec_offsets)
    enc_back_masks = build_masks(places, doc_ends, stream_len, enc_back)
    dec_back_masks = build_masks(places, doc_ends, stream_len, dec_back)
    enc_reach = max(enc_offsets)
    dec_reach = -min(dec_offsets)

    wide_shape = (micro, rows, width)
    inner_shape = (micro, rows, inner_width)
    unit = 2 * micro * rows * width * inner_width
    tap_unit = 2 * micro * rows * inner_width * inner_width

    def enter_body(*refs):
        enter_encoder_kernel(entry_origins, spacing, *refs)

    landed, copies = landing(project_pieces)
    enc_wide, dec_columns = move(enc_spreads, [], (enc_wide, dec_columns))
    dec_columns += along_fsdp(dec_columns[0], range(far_half, fsdp_count))[1:]
    dec_spreads = spread_pair(dec_columns)
    entered_shapes = [(wide_shape, BF16), (inner_shape, F32), (inner_shape, BF16)]
    first_e, hidden_e, second_e, enc_project = call(
        enter_body,
        micro,
        [stream],
        [enc_wide, enc_inner],
        entered_shapes,
        [((width, inner_width), BF16)],
        [landed],
        unit,
        project_pieces,
        place,
        copies,
    )
    tail, head = second_e[:, rows - enc_reach :], second_e[:, :enc_reach]
    while dec_spreads[0].step < len(dec_spreads[0].bits) - 2:
        move(dec_spreads, [])
    tail, head = move(dec_spreads, enc_spreads, after=(tail, head))
    low, high = to_next(tail), to_previous(head)
    enc_pieces, enc_origins = received(enc_spreads)

    def middle_body(*refs):
        middle_kernel(enc_offsets, counts, enc_origins, *refs)

    landed, copies = landing(enc_pieces)
    mixed_e, third_e, middle, enc_expand, enc_flat, dec_project = call(
        middle_body,
        micro,
        [second_e, low, high, enc_masks, stream],
        [enc_wide, enc_inner],
        [(inner_shape, F32), (inner_shape, BF16), (wide_shape, F32)],
        [
            ((inner_width, width), BF16),
            ((inner_width, ENC_TAPS * inner_width), BF16),
            ((width, inner_width), BF16),
        ],
        [
            ((rows + 2 * enc_reach, inner_width), BF16),
            ((rows, ENC_TAPS * inner_width), BF16),
            ((ENC_TAPS * inner_width, inner_width), BF16),
            landed,
        ],
        unit + ENC_TAPS * tap_unit,
        enc_pieces,
        place,
        copies,
    )

    def enter_decoder_body(stream_in, wide, inner, project, *refs):
        enter_kernel(stream_in, project, wide, inner, *refs)

    dec_inner, enc_expand = move(dec_spreads, [], (dec_inner,), (enc_expand,))
    first_d, hidden_d, second_d = call(
        enter_decoder_body,
        micro,
        [middle],
        [dec_wide, dec_inner, dec_project],
        [(wide_shape, BF16), (inner_shape, F32), (inner_shape, BF16)],
        [],
        [],
        unit,
    )
    (tail,) = move([], dec_spreads, after=(second_d[:, rows - dec_reach :],))
    dec_pieces, dec_origins = received(dec_spreads)
    low = to_next(tail)

    def turn_body(*refs):
        turn_kernel(dec_offsets, counts, dec_origins, *refs)

    landed, copies = landing(dec_pieces)
    third_d, gmixed_d, gexpand_d, dec_flat, dec_expand, turn_wide, turn_inner = call(
        turn_body,
        micro,
        [second_d, low, dec_masks, cot],
        [dec_inner],
        [(inner_shape, BF16), (inner_shape, BF16)],
        [
            ((inner_width, width), BF16),
            ((inner_width, DEC_TAPS * inner_width), BF16),
            ((inner_width, width), BF16),
            ((1, 8, width), F32),
            ((3, 8, inner_width), F32),
        ],
        [
            ((rows + dec_reach, inner_width), BF16),
            ((rows, DEC_TAPS * inner_width), BF16),
            ((rows, inner_width), F32),
            ((rows, inner_width), F32),
            ((inner_width, width), F32),
            ((DEC_TAPS * inner_width, inner_width), BF16),
            landed,
        ],
        2 * unit + DEC_TAPS * tap_unit,
        dec_pieces,
        place,
        copies,
    )
    high = to_previous(gmixed_d[:, :dec_reach])

    def packed_pair(row_total):
        part = round_up(row_total, 8 * seq_count) // seq_count
        return [((seq_count * fsdp_count // 2, part, inner_width), BF16)] * 2

    shard_part = inner_width // fsdp_count

    def decoder_back_body(*refs):
        decoder_back_kernel(dec_back, dec_reach, counts, *refs)

    ghidden_d, keep_d, send_d, conv_inner_d = call(
        decoder_back_body,
        micro,
        [gmixed_d, high, dec_back_masks, second_d, hidden_d, first_d],
        [dec_flat, dec_inner, gexpand_d],
        [(inner_shape, BF16)],
        packed_pair((DEC_TAPS + 2) * shard_part + width // fsdp_count)
        + [((3, 8, inner_width), F32)],
        [
            ((rows + dec_reach, inner_width), BF16),
            ((rows, DEC_TAPS * inner_width), BF16),
            ((rows, inner_width), F32),
            ((inner_width, DEC_TAPS * inner_width), F32),
            ((width, inner_width), F32),
        ],
        unit + 2 * DEC_TAPS * tap_unit,
        place=place,
    )

    dec_reduce = Chain(reduce_pieces(keep_d, send_d))
    dec_wide = slot(dec_wide, dec_reduce)
    gmiddle, gmixed_e, gexpand_e, link_wide, link_inner = call(
        link_back_kernel,
        micro,
        [ghidden_d, middle, cot, mixed_e, third_e],
        [dec_project, dec_wide, enc_expand, enc_inner],
        [(wide_shape, F32), (inner_shape, BF16)],
        [
            ((inner_width, width), BF16),
            ((3, 8, width), F32),
            ((3, 8, inner_width), F32),
        ],
        [
            ((rows, width), F32),
            ((rows, width), BF16),
            ((rows, inner_width), F32),
            ((inner_width, width), F32),
        ],
        3 * unit,
    )
    low = to_next(gmixed_e[:, rows - enc_reach :])
    high = to_previous(gmixed_e[:, :enc_reach])
    extended_scratch = [
        ((rows + 2 * enc_reach, inner_width), BF16),
        ((rows, ENC_TAPS * inner_width), BF16),
    ]

    def kernel_grad_body(*refs):
        encoder_kernel_grad_kernel(enc_back, enc_reach, enc_reach, counts, *refs)

    gexpand_e = slot(gexpand_e, dec_reduce)
    keep_e, send_e = call(
        kernel_grad_body,
        micro,
        [gmixed_e, low, high, enc_back_masks, second_e],
        [gexpand_e],
        [],
        packed_pair((ENC_TAPS + 2) * shard_part),
        extended_scratch + [((inner_width, ENC_TAPS * inner_width), F32)],
        ENC_TAPS * tap_unit,
        place=place,
    )

    def encoder_back_body(*refs):
        encoder_back_kernel(enc_back, enc_reach, enc_reach, counts, *refs)

    enc_reduce = Chain(reduce_pieces(keep_e, send_e))
    def encoder_back_body(*refs):
        encoder_back_kernel(enc_back, enc_reach, enc_reach, *refs)

    chains = [dec_reduce, enc_reduce]
    early = (micro + 1) // 2
    spans = [(0, early)] + ([(early, micro - early)] if micro > early else [])
    ghidden, conv_sums = (), []
    for offset, count in spans:
        enc_inner, ghidden, conv_sums = slot((enc_inner, ghidden, conv_sums), *chains)
        *ghidden, conv_part = call(
            encoder_back_body,
            count,
            [gmixed_e, low, high, enc_back_masks, hidden_e],
            [enc_flat, enc_inner],
            [(inner_shape, BF16)],
            [((3, 8, inner_width), F32)],
            extended_scratch + [((rows, inner_width), F32)],
            ENC_TAPS * tap_unit * count // micro,
            offset=offset,
            carried=ghidden,
        )
        conv_sums.append(conv_part)
    (ghidden_e,), conv_inner_e = ghidden, sum(conv_sums)

    def project_grad_body(*refs):
        project_grad_kernel(counts, *refs)

    keep_p, send_p = call(
        project_grad_body,
        micro,
        [first_e, ghidden_e],
        [],
        [],
        packed_pair(width // fsdp_count),
        [((width, inner_width), F32)],
        unit,
        place=place,
    )
    entry_reduce = Chain(reduce_pieces(keep_p, send_p))
    chains.append(entry_reduce)
    gstream, leave_sums = (), []
    for offset, count in spans:
        enc_wide, gstream, leave_sums = slot((enc_wide, gstream, leave_sums), *chains)
        *gstream, leave_wide = call(
            leave_kernel,
            count,
            [ghidden_e, stream, gmiddle],
            [enc_project, enc_wide],
            [(wide_shape, BF16)],
            [((2, 8, width), F32)],
            [((rows, width), F32)],
            unit * count // micro,
            offset=offset,
            carried=gstream,
        )
        leave_sums.append(leave_wide)

    def row_sums(entry):
        sums = jnp.sum(entry, axis=1)
        return jnp.pad(sums, ((0, 0), (0, width - sums.shape[1])))

    sums = [sum(leave_sums), link_wide, turn_wide]
    sums += [conv_inner_e, link_inner, conv_inner_d, turn_inner]
    vector_reduce = Chain(reduce_vectors(jnp.concatenate([row_sums(entry) for entry in sums])))
    chains.append(vector_reduce)
    output = ()
    for offset, count in spans:
        dec_wide, gstream, output = slot((dec_wide, gstream, output), *chains)
        output = call(
            output_kernel,
            count,
            [third_d, middle],
            [dec_expand, dec_wide],
            [(wide_shape, BF16)],
            [],
            [((rows, width), F32)],
            unit * count // micro,
            offset=offset,
            carried=output,
        )
    def own_columns(vectors):
        part = vectors.shape[1] // fsdp_count
        return lax.dynamic_slice_in_dim(vectors, own * part, part, axis=1)

    project_rows = width // fsdp_count
    scale = total_rows**-0.5
    shapes = {
        "project": (project_rows, inner_width),
        "expand": (shard_part, width),
    }

    def finish(chain, names):
        pieces, indices = chain.finish()
        layout, outs, start = [], [], 0
        for name in names:
            shape = shapes.get(name, (name, shard_part, inner_width))
            layout.append((start, name == "expand"))
            outs.append(jax.ShapeDtypeStruct(shape, F32))
            size = 1
            for extent in shape:
                size *= extent
            start += size // inner_width

        def body(*refs):
            finish_kernel(layout, scale, indices, *refs)

        whole = pl.BlockSpec(memory_space=pltpu.VMEM)
        return pl.pallas_call(
            body,
            in_specs=[pl.BlockSpec(memory_space=pltpu.SMEM)] + [whole] * len(pieces),
            out_specs=[whole] * len(outs),
            out_shape=outs,
            scratch_shapes=[pltpu.VMEM((seq_count,) + pieces[0].shape[1:], BF16)],
            compiler_params=pltpu.CompilerParams(vmem_limit_bytes=VMEM_LIMIT),
        )(place, *pieces)

    names = [["project", DEC_TAPS, "expand"], [ENC_TAPS, "expand"], ["project"]]
    finished = [None] * len(names)
    while any(chain.pending is not None for chain in chains):
        for index, entry in enumerate(names):
            if finished[index] is None and chains[index].pending is None:
                finished[index] = finish(chains[index], entry)
        output, finished = slot((output, finished), *chains)
    finished = [entry or finish(chain, kinds) for entry, chain, kinds in zip(finished, chains, names)]
    norm_sums = [0.5, 0.5, 1.0]
    shares = jnp.array(norm_sums[:2] + norm_sums + [1.0] + norm_sums * 4, F32)
    sums = vector_reduce.finish() * (shares * factor)[:, None]
    wide_sums = sums[:6]
    order = [wide_sums[:2], wide_sums[4:5], wide_sums[2:4], wide_sums[5:]]
    wide_own = own_columns(jnp.concatenate(order))
    inner_own = own_columns(sums[6:, :inner_width])

    def vectors(wide_rows, inner_rows):
        widegain = wide_rows[0]
        wideshift = wide_rows[1:3]
        gains = jnp.stack([inner_rows[0], inner_rows[3]])
        shifts = jnp.stack([inner_rows[1], inner_rows[4], inner_rows[2], inner_rows[5]])
        return widegain, gains, wideshift, shifts

    (gproject_d, gkernel_d, gexpand_d), (gkernel_e, gexpand_e), (gproject_e,) = finished
    return (
        output[0][:, None],
        gstream[0][:, None],
        gproject_e,
        gkernel_e,
        gexpand_e,
        *vectors(wide_own[:3], inner_own[:6]),
        gproject_d,
        gkernel_d,
        gexpand_d,
        *vectors(wide_own[3:], inner_own[6:]),
    )


def solution(mesh):
    tokens = P(None, "fsdp", "seq", None)
    weights = (
        P("fsdp", None),
        P(None, "fsdp", None),
        P("fsdp", None),
        P("fsdp"),
        P(None, "fsdp"),
        P(None, "fsdp"),
        P(None, "fsdp"),
    )
    return jax.shard_map(
        local,
        mesh=mesh,
        in_specs=(tokens, P(None, "fsdp", None), tokens) + weights + weights,
        out_specs=(tokens, tokens) + weights + weights,
        check_vma=False,
    )
```

```python
import jax
import jax.numpy as jnp
from jax import lax
from jax.experimental import pallas as pl
from jax.experimental.pallas import tpu as pltpu
from jax.sharding import PartitionSpec as P

ENC_TAPS = 5
ENC_DILATION = 8
DEC_TAPS = 3
DEC_DILATION = 16
EPSILON = 1e-05
CHUNK = 48
VMEM_LIMIT = 60 * 1024 * 1024

BF16 = jnp.bfloat16
F32 = jnp.float32
NN = (((1,), (0,)), ((), ()))
NT = (((1,), (1,)), ((), ()))
TN = (((0,), (0,)), ((), ()))


def dot(left, right, dims):
    return lax.dot_general(left, right, dims, preferred_element_type=F32)


def tap_offsets(encoder):
    if encoder:
        return [(tap - ENC_TAPS // 2) * ENC_DILATION for tap in range(ENC_TAPS)]
    return [(tap - DEC_TAPS + 1) * DEC_DILATION for tap in range(DEC_TAPS)]


def normalized(values):
    average = jnp.mean(values, axis=-1, keepdims=True)
    centred = values - average
    scale = lax.rsqrt(jnp.mean(centred * centred, axis=-1, keepdims=True) + EPSILON)
    return centred * scale, scale


def norm_silu(values, gain, shift):
    unit, _ = normalized(values)
    half = unit * gain + shift
    return half * (1.0 + jnp.tanh(half))


def norm_silu_back(values, gain, shift, grad):
    unit, scale = normalized(values)
    half = unit * gain + shift
    slope = jnp.tanh(half)
    grad_inner = grad * ((1.0 + slope) * (1.0 + half * (1.0 - slope)))
    grad_unit = grad_inner * gain
    along = jnp.mean(grad_unit * unit, axis=-1, keepdims=True)
    level = jnp.mean(grad_unit, axis=-1, keepdims=True)
    grad_values = scale * (grad_unit - level - unit * along)
    return grad_values, grad_inner * unit, grad_inner


def fold_rows(values):
    total = values[0:8]
    for start in range(8, values.shape[0], 8):
        total = total + values[start : start + 8]
    return total


def by_chunks(row_count, body):
    for start in range(0, row_count, CHUNK):
        body(pl.ds(start, CHUNK))


def clear_first(*refs):
    @pl.when(pl.program_id(0) == 0)
    def _():
        for ref in refs:
            ref[...] = jnp.zeros_like(ref)


def at_last(body):
    pl.when(pl.program_id(0) == pl.num_programs(0) - 1)(body)


def fill_columns(columns, extended, masks, offsets, front, row_count):
    width = extended.shape[-1]
    for tap, offset in enumerate(offsets):
        window = extended[front + offset : front + offset + row_count, :]
        if offset != 0:
            window = window * masks[:, tap : tap + 1]
        columns[:, tap * width : (tap + 1) * width] = window


def enter_kernel(stream, project, wide, inner, first, hidden, second):
    row_count = stream.shape[0]

    def make_first(rows):
        values = stream[rows, :].astype(F32)
        first[rows, :] = norm_silu(values, wide[0:1, :], wide[1:2, :]).astype(BF16)

    by_chunks(row_count, make_first)
    hidden[...] = dot(first[...], project[...], NN) + inner[4:5, :]

    def make_second(rows):
        second[rows, :] = norm_silu(hidden[rows, :], inner[0:1, :], inner[2:3, :]).astype(BF16)

    by_chunks(row_count, make_second)


def fetch(sources, spots, target, semaphores):
    copies = [
        pltpu.make_async_copy(source, target.at[spot], semaphores.at[index])
        for index, (source, spot) in enumerate(zip(sources, spots))
    ]
    for copy in copies:
        copy.start()
    for copy in copies:
        copy.wait()


def fetch_shards(place, own, parts, pieces, origins, landed, semaphores):
    sources, spots = [], []
    for piece, entries in zip(pieces, origins):
        for index, (far, differs) in enumerate(entries):
            sources.append(piece.at[index])
            spots.append((place[0] ^ far) * parts + (own ^ differs))
    fetch(sources, spots, landed, semaphores)


class Shards:
    def __init__(self, landed, fsdp_count):
        self.landed, self.fsdp_count = landed, fsdp_count
        self.seq_count = landed.shape[0] // fsdp_count

    def spread(self, shard, start, rows, write):
        part, done = self.landed.shape[1], 0
        while done < rows:
            owner, local = (start + done) // part, (start + done) % part
            size = min(rows - done, part - local)
            write(done, self.landed[shard * self.seq_count + owner, local : local + size, :])
            done += size


def enter_encoder_kernel(origins, spacing, place, stream, *refs):
    pieces, refs = refs[:-8], refs[-8:]
    wide, inner, first, hidden, second, project, landed, semaphores = refs

    @pl.when(pl.program_id(0) == 0)
    def _():
        fetch_shards(place, place[1], PARTS, pieces, origins, landed, semaphores)
        shard_rows = project.shape[0] * PARTS // landed.shape[0]
        part = shard_rows - (PARTS - 1) * spacing
        for index in range(landed.shape[0]):
            start = index // PARTS * shard_rows + index % PARTS * spacing
            project[start : start + part, :] = landed[index, :part, :]

    enter_kernel(stream, project, wide, inner, first, hidden, second)


def unpack_kernel(shards, start, taps, kernel, flat):
    width = flat.shape[0]
    part = width // shards.fsdp_count
    for own in range(shards.fsdp_count):
        for tap in range(taps):

            def write(done, block):
                row = own * part + done
                size = block.shape[0]
                kernel[tap * width + row : tap * width + row + size, :] = block
                flat[row : row + size, tap * width : (tap + 1) * width] = block

            shards.spread(own, start + tap * part, part, write)


def unpack_expand(shards, start, expand):
    width = expand.shape[1] // 2
    part = expand.shape[0] // shards.fsdp_count
    for own in range(shards.fsdp_count):
        for half in range(2):

            def write(done, block):
                row = own * part + done
                expand[row : row + block.shape[0], half * width : (half + 1) * width] = block

            shards.spread(own, start + half * part, part, write)


def unpack_rows(shards, start, whole):
    part = whole.shape[0] // shards.fsdp_count
    for own in range(shards.fsdp_count):

        def write(done, block):
            row = own * part + done
            whole[row : row + block.shape[0], :] = block

        shards.spread(own, start, part, write)


def middle_kernel(offsets, counts, origins, place, second_in, low, high, masks, stream, *refs):
    pieces, refs = refs[:-13], refs[-13:]
    enc_wide, enc_inner, mixed, third, middle, expand, flat, project = refs[:8]
    extended, columns, kernel, landed, semaphores = refs[8:]
    row_count = stream.shape[0]
    front = low.shape[0]

    @pl.when(pl.program_id(0) == 0)
    def _():
        seq_count, fsdp_count = counts
        fetch_shards(place, place[2], seq_count, pieces, origins, landed, semaphores)
        shards = Shards(landed, fsdp_count)
        unpack_kernel(shards, 0, len(offsets), kernel, flat)
        start = kernel.shape[0] // fsdp_count
        unpack_expand(shards, start, expand)
        unpack_rows(shards, start + expand.shape[0] * 2 // fsdp_count, project)

    extended[:front, :] = low[...]
    extended[front : front + row_count, :] = second_in[...]
    extended[front + row_count :, :] = high[...]
    fill_columns(columns, extended, masks, offsets, front, row_count)
    mixed[...] = dot(columns[...], kernel[...], NN) + enc_inner[5:6, :]

    def make_third(rows):
        third[rows, :] = norm_silu(mixed[rows, :], enc_inner[1:2, :], enc_inner[3:4, :]).astype(
            BF16
        )

    by_chunks(row_count, make_third)
    middle[...] = dot(third[...], expand[...], NN)

    def make_middle(rows):
        branch = middle[rows, :] + enc_wide[2:3, :]
        middle[rows, :] = stream[rows, :].astype(F32) + branch

    by_chunks(row_count, make_middle)


def turn_kernel(offsets, counts, origins, place, second, low, masks, cotangent, *refs):
    pieces, refs = refs[:-16], refs[-16:]
    inner, third, grad_mixed, grad_expand, flat, expand, sums_wide, sums_inner = refs[:8]
    extended, columns, mixed, grad_third, total, kernel, landed, semaphores = refs[8:]
    row_count = cotangent.shape[0]
    front = low.shape[0]
    clear_first(total, sums_wide, sums_inner)

    @pl.when(pl.program_id(0) == 0)
    def _():
        seq_count, fsdp_count = counts
        fetch_shards(place, place[2], seq_count, pieces, origins, landed, semaphores)
        shards = Shards(landed, fsdp_count)
        unpack_kernel(shards, 0, len(offsets), kernel, flat)
        unpack_expand(shards, kernel.shape[0] // fsdp_count, expand)

    extended[:front, :] = low[...]
    extended[front : front + row_count, :] = second[...]
    fill_columns(columns, extended, masks, offsets, front, row_count)
    mixed[...] = dot(columns[...], kernel[...], NN) + inner[5:6, :]

    def make_third(rows):
        third[rows, :] = norm_silu(mixed[rows, :], inner[1:2, :], inner[3:4, :]).astype(BF16)

    by_chunks(row_count, make_third)
    grad_third[...] = dot(cotangent[...], expand[...], NT)

    def add_cotangent(rows):
        sums_wide[0] += fold_rows(cotangent[rows, :].astype(F32))

    by_chunks(row_count, add_cotangent)

    def make_grad(rows):
        grad, gain_part, shift_part = norm_silu_back(
            mixed[rows, :], inner[1:2, :], inner[3:4, :], grad_third[rows, :]
        )
        rounded = grad.astype(BF16)
        grad_mixed[rows, :] = rounded
        sums_inner[0] += fold_rows(gain_part)
        sums_inner[1] += fold_rows(shift_part)
        sums_inner[2] += fold_rows(rounded.astype(F32))

    by_chunks(row_count, make_grad)
    total[...] += dot(third[...], cotangent[...], TN)

    @at_last
    def _():
        grad_expand[...] = total[...].astype(BF16)


def routes(seq_count):
    rest = [1 << bit for bit in range(1, seq_count.bit_length() - 1)]
    return rest[::-1], rest


def pack(place, sections, keep, send):
    seq_count, fsdp_count, part = sections.seq_count, sections.fsdp_count, keep.shape[1]
    orders = routes(seq_count)
    cells = keep.shape[0] // 2

    def write(own_core):
        for shard in range(fsdp_count):
            far = place[0] ^ shard
            half = far // (fsdp_count // 2)
            within = far % (fsdp_count // 2)
            for owner in range(seq_count):
                differs = place[2] ^ owner
                spots = []
                for order in orders:
                    spot = 0
                    for bit in order:
                        spot = spot * 2 + (differs // bit) % 2
                    spots.append(spot)
                spot = jnp.where(half == 0, spots[0], spots[1])
                spot = half * cells + spot * (fsdp_count // 2) + within
                target = keep if owner % 2 == own_core else send
                filled = 0
                for start, rows, block in sections.cut(owner * part, part):
                    target[spot, filled : filled + rows, :] = block(shard, start, rows)
                    filled += rows
                if filled < part:
                    target[spot, filled:, :] = jnp.zeros((part - filled, keep.shape[2]), BF16)

    for own_core in range(2):

        @pl.when(place[2] % 2 == own_core)
        def _():
            write(own_core)


class Sections:
    def __init__(self, seq_count, fsdp_count):
        self.seq_count, self.fsdp_count = seq_count, fsdp_count
        self.entries = []

    def add(self, rows, block):
        self.entries.append((rows, block))

    def rows_of(self, total):
        part = total.shape[0] // self.fsdp_count
        self.add(
            part,
            lambda shard, start, rows: total[
                shard * part + start : shard * part + start + rows, :
            ].astype(BF16),
        )

    def kernel(self, total, taps):
        part, width = total.shape[0] // self.fsdp_count, total.shape[1] // taps
        for tap in range(taps):
            self.add(
                part,
                lambda shard, start, rows, tap=tap: total[
                    shard * part + start : shard * part + start + rows,
                    tap * width : (tap + 1) * width,
                ].astype(BF16),
            )

    def cut(self, first, rows):
        found, begin = [], 0
        for length, block in self.entries:
            low, high = max(first, begin), min(first + rows, begin + length)
            if low < high:
                found.append((low - begin, high - low, block))
            begin += length
        return found


def back_columns(offsets, front, back, grad_mixed, low, high, masks, extended, columns):
    row_count = grad_mixed.shape[0]
    if front:
        extended[:front, :] = low[...]
    extended[front : front + row_count, :] = grad_mixed[...]
    if back:
        extended[front + row_count :, :] = high[...]
    fill_columns(columns, extended, masks, offsets, front, row_count)


def hidden_grad(hidden, inner, grad_second, grad_hidden, sums_inner):
    def make_grad(rows):
        grad, gain_part, shift_part = norm_silu_back(
            hidden[rows, :], inner[0:1, :], inner[2:3, :], grad_second[rows, :]
        )
        rounded = grad.astype(BF16)
        grad_hidden[rows, :] = rounded
        sums_inner[0] += fold_rows(gain_part)
        sums_inner[1] += fold_rows(shift_part)
        sums_inner[2] += fold_rows(rounded.astype(F32))

    by_chunks(hidden.shape[0], make_grad)


def decoder_back_kernel(
    offsets,
    back,
    counts,
    place,
    grad_mixed,
    high,
    masks,
    second,
    hidden,
    first,
    flat,
    inner,
    grad_expand,
    grad_hidden,
    keep,
    send,
    sums_inner,
    extended,
    columns,
    grad_second,
    total_kernel,
    total_project,
):
    clear_first(total_kernel, total_project, sums_inner)
    back_columns(offsets, 0, back, grad_mixed, None, high, masks, extended, columns)
    grad_second[...] = dot(columns[...], flat[...], NT)
    hidden_grad(hidden, inner, grad_second, grad_hidden, sums_inner)
    total_kernel[...] += dot(second[...], columns[...], TN)
    total_project[...] += dot(first[...], grad_hidden[...], TN)

    @at_last
    def _():
        sections = Sections(*counts)
        sections.rows_of(total_project)
        sections.kernel(total_kernel, len(offsets))
        sections.kernel(grad_expand, 2)
        pack(place, sections, keep, send)


def encoder_kernel_grad_kernel(
    offsets,
    front,
    back,
    counts,
    place,
    grad_mixed,
    low,
    high,
    masks,
    second,
    grad_expand,
    keep,
    send,
    extended,
    columns,
    total_kernel,
):
    clear_first(total_kernel)
    back_columns(offsets, front, back, grad_mixed, low, high, masks, extended, columns)
    total_kernel[...] += dot(second[...], columns[...], TN)

    @at_last
    def _():
        sections = Sections(*counts)
        sections.kernel(total_kernel, len(offsets))
        sections.kernel(grad_expand, 2)
        pack(place, sections, keep, send)


def encoder_back_kernel(
    offsets,
    front,
    back,
    grad_mixed,
    low,
    high,
    masks,
    hidden,
    flat,
    inner,
    grad_hidden,
    sums_inner,
    extended,
    columns,
    grad_second,
):
    clear_first(sums_inner)
    back_columns(offsets, front, back, grad_mixed, low, high, masks, extended, columns)
    grad_second[...] = dot(columns[...], flat[...], NT)
    hidden_grad(hidden, inner, grad_second, grad_hidden, sums_inner)


def project_grad_kernel(counts, place, first, grad_hidden, keep, send, total):
    clear_first(total)
    total[...] += dot(first[...], grad_hidden[...], TN)

    @at_last
    def _():
        sections = Sections(*counts)
        sections.rows_of(total)
        pack(place, sections, keep, send)


def link_back_kernel(
    grad_hidden,
    middle,
    cotangent,
    mixed,
    third,
    project,
    dec_wide,
    expand,
    enc_inner,
    grad_middle,
    grad_mixed,
    grad_expand,
    sums_wide,
    sums_inner,
    grad_first,
    branch,
    grad_third,
    total,
):
    row_count = middle.shape[0]
    clear_first(total, sums_wide, sums_inner)
    grad_first[...] = dot(grad_hidden[...], project[...], NT)

    def make_branch(rows):
        grad, gain_part, shift_part = norm_silu_back(
            middle[rows, :], dec_wide[0:1, :], dec_wide[1:2, :], grad_first[rows, :]
        )
        sums_wide[0] += fold_rows(gain_part)
        sums_wide[1] += fold_rows(shift_part)
        grad = cotangent[rows, :].astype(F32) + grad
        grad_middle[rows, :] = grad
        rounded = grad.astype(BF16)
        branch[rows, :] = rounded
        sums_wide[2] += fold_rows(rounded.astype(F32))

    by_chunks(row_count, make_branch)
    grad_third[...] = dot(branch[...], expand[...], NT)

    def make_grad(rows):
        grad, gain_part, shift_part = norm_silu_back(
            mixed[rows, :], enc_inner[1:2, :], enc_inner[3:4, :], grad_third[rows, :]
        )
        rounded = grad.astype(BF16)
        grad_mixed[rows, :] = rounded
        sums_inner[0] += fold_rows(gain_part)
        sums_inner[1] += fold_rows(shift_part)
        sums_inner[2] += fold_rows(rounded.astype(F32))

    by_chunks(row_count, make_grad)
    total[...] += dot(third[...], branch[...], TN)

    @at_last
    def _():
        grad_expand[...] = total[...].astype(BF16)


def output_kernel(third, middle, expand, wide, output, branch):
    branch[...] = dot(third[...], expand[...], NN)

    def make_output(rows):
        values = middle[rows, :] + (branch[rows, :] + wide[2:3, :])
        output[rows, :] = values.astype(BF16)

    by_chunks(middle.shape[0], make_output)


def leave_kernel(
    grad_hidden, stream, grad_middle, project, wide, grad_stream, sums_wide, grad_first
):
    row_count = stream.shape[0]
    clear_first(sums_wide)
    grad_first[...] = dot(grad_hidden[...], project[...], NT)

    def make_grad(rows):
        grad, gain_part, shift_part = norm_silu_back(
            stream[rows, :].astype(F32), wide[0:1, :], wide[1:2, :], grad_first[rows, :]
        )
        sums_wide[0] += fold_rows(gain_part)
        sums_wide[1] += fold_rows(shift_part)
        grad_stream[rows, :] = (grad_middle[rows, :] + grad).astype(BF16)

    by_chunks(row_count, make_grad)


def finish_kernel(layout, factor, indices, place, *refs):
    count = len(indices)
    pieces, outs, landed = refs[:count], refs[count:-1], refs[-1]
    part = landed.shape[1]
    for piece, entries in zip(pieces, indices):
        for spot, index in enumerate(entries):
            landed[place[2] ^ index] = piece[spot]

    def write(out, where, columns, start, rows):
        done = 0
        while done < rows:
            owner, local = (start + done) // part, (start + done) % part
            size = min(rows - done, part - local)
            block = landed[owner, local : local + size, :].astype(F32) * factor
            if where is None:
                out[done : done + size, columns] = block
            else:
                out[where, done : done + size, :] = block
            done += size

    for out, (start, halves) in zip(outs, layout):
        width = landed.shape[2]
        if halves:
            for half in range(2):
                columns = slice(half * width, (half + 1) * width)
                write(out, None, columns, start + half * out.shape[0], out.shape[0])
        elif len(out.shape) == 3:
            for tap in range(out.shape[0]):
                write(out, tap, None, start + tap * out.shape[1], out.shape[1])
        else:
            write(out, None, slice(0, width), start, out.shape[0])


def stepped(array, offset):
    rest = (0,) * (array.ndim - 1)
    return pl.BlockSpec((None,) + array.shape[1:], lambda step: (step + offset,) + rest)


def held(array):
    zeros = (0,) * array.ndim
    return pl.BlockSpec(array.shape, lambda step: zeros, pipeline_mode=pl.Buffered(1))


def call(
    body,
    steps,
    moving,
    fixed,
    outs,
    sums,
    scratch,
    flops,
    loose=(),
    place=None,
    semaphores=0,
    offset=0,
    carried=(),
):
    out_shapes = [jax.ShapeDtypeStruct(shape, kind) for shape, kind in outs]
    sum_shapes = [jax.ShapeDtypeStruct(shape, kind) for shape, kind in sums]
    operands = list(moving) + list(loose) + list(fixed)
    traffic = sum(
        entry.size * entry.dtype.itemsize for entry in operands + out_shapes + sum_shapes
    )
    in_specs = [stepped(entry, offset) for entry in moving]
    in_specs += [pl.BlockSpec(memory_space=pl.ANY) for _ in loose]
    in_specs += [held(entry) for entry in fixed]
    if place is not None:
        operands = [place] + operands
        in_specs = [pl.BlockSpec(memory_space=pltpu.SMEM)] + in_specs
    count = len(operands)
    operands += list(carried)
    in_specs += [pl.BlockSpec(memory_space=pl.ANY) for _ in carried]
    scratch_shapes = [pltpu.VMEM(shape, kind) for shape, kind in scratch]
    if semaphores:
        scratch_shapes.append(pltpu.SemaphoreType.DMA((semaphores,)))

    def kernel(*refs):
        body(*refs[:count], *refs[count + len(carried) :])

    return pl.pallas_call(
        kernel,
        grid=(steps,),
        in_specs=in_specs,
        out_specs=[stepped(entry, offset) for entry in out_shapes]
        + [held(entry) for entry in sum_shapes],
        out_shape=out_shapes + sum_shapes,
        scratch_shapes=scratch_shapes,
        input_output_aliases={count + index: index for index in range(len(carried))},
        compiler_params=pltpu.CompilerParams(
            dimension_semantics=("arbitrary",), vmem_limit_bytes=VMEM_LIMIT
        ),
        cost_estimate=pl.CostEstimate(flops=flops, bytes_accessed=traffic, transcendentals=0),
    )(*operands)


def owners(places, doc_ends):
    return jnp.sum((places[..., None] >= doc_ends[:, None, :]).astype(jnp.int32), axis=-1)


def build_masks(places, doc_ends, stream_len, offsets):
    own_doc = owners(places[None, :], doc_ends)
    columns = []
    for offset in offsets:
        partner = places + offset
        inside = (partner >= 0) & (partner < stream_len)
        columns.append(inside[None, :] & (owners(partner[None, :], doc_ends) == own_doc))
    return jnp.stack(columns, axis=-1).astype(BF16)


def to_next(block):
    count = lax.axis_size("seq")
    return lax.ppermute(block, "seq", [(i, i + 1) for i in range(count - 1)])


def to_previous(block):
    count = lax.axis_size("seq")
    return lax.ppermute(block, "seq", [(i + 1, i) for i in range(count - 1)])


def exchanged(block, axis, bit):
    return lax.ppermute(block, axis, [(i, i ^ bit) for i in range(lax.axis_size(axis))])


def round_up(value, unit):
    return -(-value // unit) * unit


def padded(block, rows):
    return jnp.pad(block, ((0, rows - block.shape[0]), (0, 0)))


class Chain:
    def __init__(self, steps):
        self.steps, self.result = steps, None
        self.pending = next(steps)

    def advance(self, arrays=None):
        try:
            self.pending = self.steps.send(self.pending if arrays is None else arrays)
        except StopIteration as stop:
            self.pending, self.result = None, stop.value
        return self

    def finish(self):
        while self.pending is not None:
            self.advance()
        return self.result


def slot(operand, *chains):
    live = [chain for chain in chains if chain.pending is not None]
    operand, arrays = lax.optimization_barrier((operand, [chain.pending for chain in live]))
    for chain, pending in zip(live, arrays):
        chain.advance(pending)
    return operand


PARTS = 4


def half_spacing(rows):
    part = round_up(rows // PARTS, 16)
    return part, (rows - part) // (PARTS - 1)


def tiled(block):
    return block.reshape(block.shape[0] // 8, 8, block.shape[1])


class Spread:
    def __init__(self, columns, fars, bits):
        self.parts = [jnp.stack(columns)]
        self.bits, self.step = bits, 0
        self.origins = [(far, 0) for far in fars]
        self.arrays, self.all_origins = [], []

    def moved(self, entries, bit):
        return [(far, differs ^ bit) for far, differs in entries]

    def advance(self, block):
        bit = self.bits[self.step]
        other = exchanged(block, "seq", bit)
        more = self.moved(self.origins, bit)
        self.step += 1
        if self.step < len(self.bits):
            self.parts = [block, other]
            self.origins = self.origins + more
        else:
            self.arrays = [other, block, exchanged(block, "seq", 1)]
            self.all_origins = [more, self.origins, self.moved(self.origins, 1)]

    def cross(self, arrays):
        self.arrays = arrays + [exchanged(arrays[0], "seq", 1)]
        self.all_origins.append(self.moved(self.all_origins[0], 1))


def move(spreads, crossing, before=(), after=()):
    parts, arrays, after = lax.optimization_barrier(
        ([entry.parts for entry in spreads], [entry.arrays for entry in crossing], after)
    )
    blocks = [jnp.concatenate(pair, axis=0) if len(pair) > 1 else pair[0] for pair in parts]
    blocks, arrays, before = lax.optimization_barrier((blocks, arrays, before))
    for entry, block in zip(spreads, blocks):
        entry.advance(block)
    for entry, own in zip(crossing, arrays):
        entry.cross(own)
    return tuple(before) + tuple(after)


def in_progress(spreads):
    return spreads[0].step < len(spreads[0].bits) - 1


def received(spreads):
    arrays = [
        array.reshape(array.shape[0], -1, array.shape[-1])
        for entry in spreads
        for array in entry.arrays
    ]
    origins = [entries for entry in spreads for entries in entry.all_origins]
    return arrays, origins


def along_fsdp(block, fars=None):
    fars = range(1, lax.axis_size("fsdp")) if fars is None else fars
    return [block] + [exchanged(block, "fsdp", far) for far in fars]


def spread_pair(columns):
    orders = routes(lax.axis_size("seq"))
    middle = len(columns) // 2
    return [
        Spread(columns[:middle], range(middle), orders[0]),
        Spread(columns[middle:], range(middle, len(columns)), orders[1]),
    ]


def half_piece(shard):
    part, spacing = half_spacing(shard.shape[0])
    own = lax.axis_index("seq") & (PARTS - 1)
    return lax.dynamic_slice_in_dim(shard, own * spacing, part, axis=0)


def full_piece(shard):
    seq_count = lax.axis_size("seq")
    part = round_up(shard.shape[0], 8 * seq_count) // seq_count
    return tiled(
        lax.dynamic_slice_in_dim(
            padded(shard, part * seq_count), lax.axis_index("seq") * part, part, axis=0
        )
    )


def add_low(*blocks):
    if len(blocks) == 2:
        return blocks[0] + blocks[1]
    total = blocks[0].astype(F32)
    for block in blocks[1:]:
        total = total + block.astype(F32)
    return total.astype(BF16)


def reduce_pieces(keep, send):
    seq_count, fsdp_count = lax.axis_size("seq"), lax.axis_size("fsdp")
    shape = (2, -1, fsdp_count // 2) + keep.shape[1:]
    (send,) = yield [send]
    parts = (keep.reshape(shape), exchanged(send, "seq", 1).reshape(shape))
    orders = routes(seq_count)
    terms = [[entry[half] for entry in parts] for half in range(2)]
    for step in range(len(orders[0])):
        size = terms[0][0].shape[0] // 2
        leaving = [add_low(*[term[size:] for term in entries]) for entries in terms]
        leaving = yield leaving
        terms = [
            [term[:size] for term in entries] + [exchanged(block, "seq", order[step])]
            for entries, block, order in zip(terms, leaving, orders)
        ]
    columns = []
    for entries in terms:
        columns += [[term[0, within] for term in entries] for within in range(fsdp_count // 2)]
    leaving = yield [add_low(*columns[far]) for far in range(1, fsdp_count)]
    arrived = [exchanged(block, "fsdp", far + 1) for far, block in enumerate(leaving)]
    block, indices = add_low(*columns[0], *arrived)[None], [0]
    for bit in orders[1]:
        (block,) = yield [block]
        block = jnp.concatenate([block, exchanged(block, "seq", bit)], axis=0)
        indices = indices + [index ^ bit for index in indices]
    (block,) = yield [block]
    return [block, exchanged(block, "seq", 1)], [indices, [index ^ 1 for index in indices]]


def reduce_vectors(vectors):
    for axis in ("seq", "fsdp"):
        bit = 1
        while bit < lax.axis_size(axis):
            (vectors,) = yield [vectors]
            vectors = vectors + exchanged(vectors, axis, bit)
            bit *= 2
    return vectors


def local(
    characters,
    lengths,
    cotangent,
    encproject,
    enckernel,
    encexpand,
    encwidegain,
    encgains,
    encwideshift,
    encshifts,
    decproject,
    deckernel,
    decexpand,
    decwidegain,
    decgains,
    decwideshift,
    decshifts,
):
    micro, _, rows, width = characters.shape
    inner_width = encproject.shape[1]
    seq_count = lax.axis_size("seq")
    fsdp_count = lax.axis_size("fsdp")
    stream_len = rows * seq_count
    total_rows = micro * stream_len * fsdp_count
    factor = 1.0 / jnp.sqrt(jnp.float32(total_rows))
    stream = characters[:, 0]
    cot = cotangent[:, 0]

    seq_index = lax.axis_index("seq")
    place = jnp.stack([lax.axis_index("fsdp"), seq_index & (PARTS - 1), seq_index])
    place = place.astype(jnp.int32)
    def rows_of(kernel):
        return kernel.reshape(-1, kernel.shape[2])

    def halves(expand):
        return [expand[:, :inner_width], expand[:, inner_width:]]

    wide_local = [encwidegain[None], encwideshift, decwidegain[None], decwideshift]
    wide_local = jnp.concatenate(wide_local, axis=0)
    inner_local = jnp.concatenate([encgains, encshifts, decgains, decshifts], axis=0)
    vector_local = jnp.concatenate([wide_local.reshape(-1), inner_local.reshape(-1)])
    enc_rows = jnp.concatenate([rows_of(enckernel)] + halves(encexpand) + [decproject], axis=0)
    dec_rows = jnp.concatenate([rows_of(deckernel)] + halves(decexpand), axis=0)
    _, spacing = half_spacing(encproject.shape[0])
    counts = (seq_count, fsdp_count)
    enc_own, dec_own = full_piece(enc_rows), full_piece(dec_rows)
    vector_rows = round_up(vector_local.size, 8 * inner_width) // inner_width
    vector_piece = jnp.pad(vector_local, (0, vector_rows * inner_width - vector_local.size))
    vector_piece = vector_piece.reshape(vector_rows, inner_width)
    entry_piece = jnp.concatenate([half_piece(encproject), vector_piece], axis=0)
    entry_columns = along_fsdp(tiled(entry_piece))
    entry_spread = Spread(entry_columns, range(fsdp_count), [2])
    move([entry_spread], [])
    enc_spreads = spread_pair(along_fsdp(enc_own))
    vector_shards = jnp.stack(
        [column[-vector_rows // 8 :].reshape(-1)[: vector_local.size] for column in entry_columns]
    )
    own = lax.axis_index("fsdp")
    vector_shards = jnp.stack(
        [
            lax.dynamic_index_in_dim(vector_shards, own ^ shard, 0, keepdims=False)
            for shard in range(fsdp_count)
        ]
    ).astype(F32)

    def whole_vectors(shards, like):
        cut = shards.reshape((fsdp_count,) + like.shape)
        return jnp.transpose(cut, (1, 0, 2)).reshape(like.shape[0], -1)

    wides = whole_vectors(vector_shards[:, : wide_local.size], wide_local)
    inners = whole_vectors(vector_shards[:, wide_local.size :], inner_local)
    wides = wides * jnp.array([0.5, 0.5, 1.0] * 2, F32)[:, None]
    inners = inners * jnp.array(([0.5] * 4 + [1.0] * 2) * 2, F32)[:, None]
    enc_wide, dec_wide = wides[:3], wides[3:]
    enc_inner, dec_inner = inners[:6], inners[6:]

    far_half = fsdp_count // 2 + 1
    (dec_own,) = move(enc_spreads, [entry_spread], (dec_own,))
    dec_columns = along_fsdp(dec_own, range(1, far_half))
    project_pieces, entry_origins = received([entry_spread])
    while in_progress(enc_spreads):
        move(enc_spreads, [])

    def landing(pieces):
        count = sum(piece.shape[0] for piece in pieces)
        return ((count,) + pieces[0].shape[1:], BF16), count

    places = lax.axis_index("seq") * rows + jnp.arange(rows, dtype=jnp.int32)
    doc_ends = jnp.cumsum(lengths[:, 0], axis=1)
    enc_offsets = tap_offsets(True)
    dec_offsets = tap_offsets(False)
    enc_back = [-offset for offset in enc_offsets]
    dec_back = [-offset for offset in dec_offsets]
    enc_masks = build_masks(places, doc_ends, stream_len, enc_offsets)
    dec_masks = build_masks(places, doc_ends, stream_len, dec_offsets)
    enc_back_masks = build_masks(places, doc_ends, stream_len, enc_back)
    dec_back_masks = build_masks(places, doc_ends, stream_len, dec_back)
    enc_reach = max(enc_offsets)
    dec_reach = -min(dec_offsets)

    wide_shape = (micro, rows, width)
    inner_shape = (micro, rows, inner_width)
    unit = 2 * micro * rows * width * inner_width
    tap_unit = 2 * micro * rows * inner_width * inner_width

    def enter_body(*refs):
        enter_encoder_kernel(entry_origins, spacing, *refs)

    landed, copies = landing(project_pieces)
    enc_wide, dec_columns = move(enc_spreads, [], (enc_wide, dec_columns))
    dec_columns += along_fsdp(dec_columns[0], range(far_half, fsdp_count))[1:]
    dec_spreads = spread_pair(dec_columns)
    entered_shapes = [(wide_shape, BF16), (inner_shape, F32), (inner_shape, BF16)]
    first_e, hidden_e, second_e, enc_project = call(
        enter_body,
        micro,
        [stream],
        [enc_wide, enc_inner],
        entered_shapes,
        [((width, inner_width), BF16)],
        [landed],
        unit,
        project_pieces,
        place,
        copies,
    )
    tail, head = second_e[:, rows - enc_reach :], second_e[:, :enc_reach]
    while dec_spreads[0].step < len(dec_spreads[0].bits) - 2:
        move(dec_spreads, [])
    tail, head = move(dec_spreads, enc_spreads, after=(tail, head))
    low, high = to_next(tail), to_previous(head)
    enc_pieces, enc_origins = received(enc_spreads)

    def middle_body(*refs):
        middle_kernel(enc_offsets, counts, enc_origins, *refs)

    landed, copies = landing(enc_pieces)
    mixed_e, third_e, middle, enc_expand, enc_flat, dec_project = call(
        middle_body,
        micro,
        [second_e, low, high, enc_masks, stream],
        [enc_wide, enc_inner],
        [(inner_shape, F32), (inner_shape, BF16), (wide_shape, F32)],
        [
            ((inner_width, width), BF16),
            ((inner_width, ENC_TAPS * inner_width), BF16),
            ((width, inner_width), BF16),
        ],
        [
            ((rows + 2 * enc_reach, inner_width), BF16),
            ((rows, ENC_TAPS * inner_width), BF16),
            ((ENC_TAPS * inner_width, inner_width), BF16),
            landed,
        ],
        unit + ENC_TAPS * tap_unit,
        enc_pieces,
        place,
        copies,
    )

    def enter_decoder_body(stream_in, wide, inner, project, *refs):
        enter_kernel(stream_in, project, wide, inner, *refs)

    dec_inner, enc_expand = move(dec_spreads, [], (dec_inner,), (enc_expand,))
    first_d, hidden_d, second_d = call(
        enter_decoder_body,
        micro,
        [middle],
        [dec_wide, dec_inner, dec_project],
        [(wide_shape, BF16), (inner_shape, F32), (inner_shape, BF16)],
        [],
        [],
        unit,
    )
    (tail,) = move([], dec_spreads, after=(second_d[:, rows - dec_reach :],))
    dec_pieces, dec_origins = received(dec_spreads)
    low = to_next(tail)

    def turn_body(*refs):
        turn_kernel(dec_offsets, counts, dec_origins, *refs)

    landed, copies = landing(dec_pieces)
    third_d, gmixed_d, gexpand_d, dec_flat, dec_expand, turn_wide, turn_inner = call(
        turn_body,
        micro,
        [second_d, low, dec_masks, cot],
        [dec_inner],
        [(inner_shape, BF16), (inner_shape, BF16)],
        [
            ((inner_width, width), BF16),
            ((inner_width, DEC_TAPS * inner_width), BF16),
            ((inner_width, width), BF16),
            ((1, 8, width), F32),
            ((3, 8, inner_width), F32),
        ],
        [
            ((rows + dec_reach, inner_width), BF16),
            ((rows, DEC_TAPS * inner_width), BF16),
            ((rows, inner_width), F32),
            ((rows, inner_width), F32),
            ((inner_width, width), F32),
            ((DEC_TAPS * inner_width, inner_width), BF16),
            landed,
        ],
        2 * unit + DEC_TAPS * tap_unit,
        dec_pieces,
        place,
        copies,
    )
    high = to_previous(gmixed_d[:, :dec_reach])

    def packed_pair(row_total):
        part = round_up(row_total, 8 * seq_count) // seq_count
        return [((seq_count * fsdp_count // 2, part, inner_width), BF16)] * 2

    shard_part = inner_width // fsdp_count

    def decoder_back_body(*refs):
        decoder_back_kernel(dec_back, dec_reach, counts, *refs)

    ghidden_d, keep_d, send_d, conv_inner_d = call(
        decoder_back_body,
        micro,
        [gmixed_d, high, dec_back_masks, second_d, hidden_d, first_d],
        [dec_flat, dec_inner, gexpand_d],
        [(inner_shape, BF16)],
        packed_pair((DEC_TAPS + 2) * shard_part + width // fsdp_count)
        + [((3, 8, inner_width), F32)],
        [
            ((rows + dec_reach, inner_width), BF16),
            ((rows, DEC_TAPS * inner_width), BF16),
            ((rows, inner_width), F32),
            ((inner_width, DEC_TAPS * inner_width), F32),
            ((width, inner_width), F32),
        ],
        unit + 2 * DEC_TAPS * tap_unit,
        place=place,
    )

    dec_reduce = Chain(reduce_pieces(keep_d, send_d))
    dec_wide = slot(dec_wide, dec_reduce)
    gmiddle, gmixed_e, gexpand_e, link_wide, link_inner = call(
        link_back_kernel,
        micro,
        [ghidden_d, middle, cot, mixed_e, third_e],
        [dec_project, dec_wide, enc_expand, enc_inner],
        [(wide_shape, F32), (inner_shape, BF16)],
        [
            ((inner_width, width), BF16),
            ((3, 8, width), F32),
            ((3, 8, inner_width), F32),
        ],
        [
            ((rows, width), F32),
            ((rows, width), BF16),
            ((rows, inner_width), F32),
            ((inner_width, width), F32),
        ],
        3 * unit,
    )
    low = to_next(gmixed_e[:, rows - enc_reach :])
    high = to_previous(gmixed_e[:, :enc_reach])
    extended_scratch = [
        ((rows + 2 * enc_reach, inner_width), BF16),
        ((rows, ENC_TAPS * inner_width), BF16),
    ]

    def kernel_grad_body(*refs):
        encoder_kernel_grad_kernel(enc_back, enc_reach, enc_reach, counts, *refs)

    gexpand_e = slot(gexpand_e, dec_reduce)
    keep_e, send_e = call(
        kernel_grad_body,
        micro,
        [gmixed_e, low, high, enc_back_masks, second_e],
        [gexpand_e],
        [],
        packed_pair((ENC_TAPS + 2) * shard_part),
        extended_scratch + [((inner_width, ENC_TAPS * inner_width), F32)],
        ENC_TAPS * tap_unit,
        place=place,
    )

    def encoder_back_body(*refs):
        encoder_back_kernel(enc_back, enc_reach, enc_reach, counts, *refs)

    enc_reduce = Chain(reduce_pieces(keep_e, send_e))
    def encoder_back_body(*refs):
        encoder_back_kernel(enc_back, enc_reach, enc_reach, *refs)

    chains = [dec_reduce, enc_reduce]
    early = (micro + 1) // 2
    spans = [(0, early)] + ([(early, micro - early)] if micro > early else [])
    ghidden, conv_sums = (), []
    for offset, count in spans:
        enc_inner, ghidden, conv_sums = slot((enc_inner, ghidden, conv_sums), *chains)
        *ghidden, conv_part = call(
            encoder_back_body,
            count,
            [gmixed_e, low, high, enc_back_masks, hidden_e],
            [enc_flat, enc_inner],
            [(inner_shape, BF16)],
            [((3, 8, inner_width), F32)],
            extended_scratch + [((rows, inner_width), F32)],
            ENC_TAPS * tap_unit * count // micro,
            offset=offset,
            carried=ghidden,
        )
        conv_sums.append(conv_part)
    (ghidden_e,), conv_inner_e = ghidden, sum(conv_sums)

    def project_grad_body(*refs):
        project_grad_kernel(counts, *refs)

    keep_p, send_p = call(
        project_grad_body,
        micro,
        [first_e, ghidden_e],
        [],
        [],
        packed_pair(width // fsdp_count),
        [((width, inner_width), F32)],
        unit,
        place=place,
    )
    entry_reduce = Chain(reduce_pieces(keep_p, send_p))
    chains.append(entry_reduce)
    gstream, leave_sums = (), []
    for offset, count in spans:
        enc_wide, gstream, leave_sums = slot((enc_wide, gstream, leave_sums), *chains)
        *gstream, leave_wide = call(
            leave_kernel,
            count,
            [ghidden_e, stream, gmiddle],
            [enc_project, enc_wide],
            [(wide_shape, BF16)],
            [((2, 8, width), F32)],
            [((rows, width), F32)],
            unit * count // micro,
            offset=offset,
            carried=gstream,
        )
        leave_sums.append(leave_wide)

    def row_sums(entry):
        sums = jnp.sum(entry, axis=1)
        return jnp.pad(sums, ((0, 0), (0, width - sums.shape[1])))

    sums = [sum(leave_sums), link_wide, turn_wide]
    sums += [conv_inner_e, link_inner, conv_inner_d, turn_inner]
    vector_reduce = Chain(reduce_vectors(jnp.concatenate([row_sums(entry) for entry in sums])))
    chains.append(vector_reduce)
    output = ()
    for offset, count in spans:
        dec_wide, gstream, output = slot((dec_wide, gstream, output), *chains)
        output = call(
            output_kernel,
            count,
            [third_d, middle],
            [dec_expand, dec_wide],
            [(wide_shape, BF16)],
            [],
            [((rows, width), F32)],
            unit * count // micro,
            offset=offset,
            carried=output,
        )
    def own_columns(vectors):
        part = vectors.shape[1] // fsdp_count
        return lax.dynamic_slice_in_dim(vectors, own * part, part, axis=1)

    project_rows = width // fsdp_count
    scale = total_rows**-0.5
    shapes = {
        "project": (project_rows, inner_width),
        "expand": (shard_part, width),
    }

    def finish(chain, names):
        pieces, indices = chain.finish()
        layout, outs, start = [], [], 0
        for name in names:
            shape = shapes.get(name, (name, shard_part, inner_width))
            layout.append((start, name == "expand"))
            outs.append(jax.ShapeDtypeStruct(shape, F32))
            size = 1
            for extent in shape:
                size *= extent
            start += size // inner_width

        def body(*refs):
            finish_kernel(layout, scale, indices, *refs)

        whole = pl.BlockSpec(memory_space=pltpu.VMEM)
        return pl.pallas_call(
            body,
            in_specs=[pl.BlockSpec(memory_space=pltpu.SMEM)] + [whole] * len(pieces),
            out_specs=[whole] * len(outs),
            out_shape=outs,
            scratch_shapes=[pltpu.VMEM((seq_count,) + pieces[0].shape[1:], BF16)],
            compiler_params=pltpu.CompilerParams(vmem_limit_bytes=VMEM_LIMIT),
        )(place, *pieces)

    names = [["project", DEC_TAPS, "expand"], [ENC_TAPS, "expand"], ["project"]]
    finished = [None] * len(names)
    while any(chain.pending is not None for chain in chains):
        for index, entry in enumerate(names):
            if finished[index] is None and chains[index].pending is None:
                finished[index] = finish(chains[index], entry)
        output, finished = slot((output, finished), *chains)
    finished = [entry or finish(chain, kinds) for entry, chain, kinds in zip(finished, chains, names)]
    norm_sums = [0.5, 0.5, 1.0]
    shares = jnp.array(norm_sums[:2] + norm_sums + [1.0] + norm_sums * 4, F32)
    sums = vector_reduce.finish() * (shares * factor)[:, None]
    wide_sums = sums[:6]
    order = [wide_sums[:2], wide_sums[4:5], wide_sums[2:4], wide_sums[5:]]
    wide_own = own_columns(jnp.concatenate(order))
    inner_own = own_columns(sums[6:, :inner_width])

    def vectors(wide_rows, inner_rows):
        widegain = wide_rows[0]
        wideshift = wide_rows[1:3]
        gains = jnp.stack([inner_rows[0], inner_rows[3]])
        shifts = jnp.stack([inner_rows[1], inner_rows[4], inner_rows[2], inner_rows[5]])
        return widegain, gains, wideshift, shifts

    (gproject_d, gkernel_d, gexpand_d), (gkernel_e, gexpand_e), (gproject_e,) = finished
    return (
        output[0][:, None],
        gstream[0][:, None],
        gproject_e,
        gkernel_e,
        gexpand_e,
        *vectors(wide_own[:3], inner_own[:6]),
        gproject_d,
        gkernel_d,
        gexpand_d,
        *vectors(wide_own[3:], inner_own[6:]),
    )


def solution(mesh):
    tokens = P(None, "fsdp", "seq", None)
    weights = (
        P("fsdp", None),
        P(None, "fsdp", None),
        P("fsdp", None),
        P("fsdp"),
        P(None, "fsdp"),
        P(None, "fsdp"),
        P(None, "fsdp"),
    )
    return jax.shard_map(
        local,
        mesh=mesh,
        in_specs=(tokens, P(None, "fsdp", None), tokens) + weights + weights,
        out_specs=(tokens, tokens) + weights + weights,
        check_vma=False,
    )
```
